256 devices in a mesh: dp: 8 (over z_lo, core), ctx: 32 (over y, z_hi, x).
Axes of the slice: x: 4, y: 4, z: 8 (z_hi: 2, z_lo: 4; z = z_hi * 4 + z_lo), core: 2. Of those that a mesh axis runs over, the one named last changes fastest.
Arguments:
- queries: bfloat16 [8, 6144, 5120], P('dp', 'ctx'), may hold values from -420 to 420
- packed_keys_values: bfloat16 [8, 6144, 2048], P('dp', 'ctx'), may hold values from -5 to 5
- cotangents: bfloat16 [8, 6144, 2, 5120], P('dp', 'ctx'), may hold values from -5 to 5
- send_rows: int32 [8, 32, 32, 7], P('dp', 'ctx'), may hold values from -1 to 191, as said below
- take_slots: int32 [8, 6144], P('dp', 'ctx'), may hold values from 0 to 223, as said below
- segment_ids: int32 [8, 6144], P('dp', 'ctx'), may hold values from 0 to 63, never falling along the last dimension, each value on 1 to 576 neighbouring positions
Outputs:
- attention_out: bfloat16 [8, 6144, 5120], P('dp', 'ctx')
- bias_curvature: float32 [5120], replicated
The draws below stay inside these ranges and needn't reach their ends.
Inputs may be any that keep to these rules, and one draw needn't show every extreme that they name: send_rows[pack, s, t] lists distinct local rows of device s first and -1 after them; over all t every local row of s is listed once; at most 7 rows from s to t, reached in every pack. take_slots[pack, t * 192 + r] = s * 7 + k names the k-th listed row of send_rows[pack, s, t]; every listed row is named once.
All inputs are finite; a program needn't handle non-finite values.
Results may differ from the reference program's by a relative error of at most 0.0055.
Values may be sent and summed in bfloat16 or wider, within the bound.
A program may use at most 128 MiB of HBM per device.

```python
import math
from functools import partial
import jax
import jax.numpy as jnp
import numpy as np
from jax import lax

QUERY_HEADS = 40
KEY_VALUE_HEADS = 8
HEAD_SIZE = 128
TOK_DEV = 192
GROUP_MOST = 4
PACK_COUNT = 8
PACK_TOKENS = 6144
SPREAD = 1
CAP = 7
SEGS = 64
DOC_MOST = 576
N_CTX = 32


def route_tables(key):
    base_count = TOK_DEV // N_CTX
    half_count = SPREAD
    key_spread, key_shift, key_rows, key_order = jax.random.split(key, 4)
    spread = jax.random.randint(key_spread, (PACK_COUNT, N_CTX // 2), 0, half_count + 1)
    spread = spread.at[:, 0].set(half_count)
    counts = jnp.concatenate([base_count + spread, base_count - spread], axis=1).astype(jnp.int32)
    shifts = jax.vmap(lambda subkey: jax.random.permutation(subkey, N_CTX))(jax.random.split(key_shift, PACK_COUNT))
    inverse = jnp.argsort(shifts, axis=1).astype(jnp.int32)
    device_index = jnp.arange(N_CTX, dtype=jnp.int32)
    offset = (device_index[None, :] - device_index[:, None]) % N_CTX
    shift_index = inverse[:, offset]
    pair_count = jnp.take_along_axis(counts, shift_index.reshape(PACK_COUNT, -1), axis=1).reshape(PACK_COUNT, N_CTX, N_CTX)
    first_row = jnp.cumsum(pair_count, axis=2) - pair_count
    orders = jax.vmap(lambda subkey: jax.random.permutation(subkey, TOK_DEV))(jax.random.split(key_rows, PACK_COUNT * N_CTX))
    orders = orders.reshape(PACK_COUNT, N_CTX, TOK_DEV).astype(jnp.int32)
    slot_number = jnp.arange(CAP, dtype=jnp.int32)
    position = first_row[..., None] + slot_number
    filled = slot_number < pair_count[..., None]
    spread_orders = jnp.broadcast_to(orders[:, :, None, :], (PACK_COUNT, N_CTX, N_CTX, TOK_DEV))
    picked = jnp.take_along_axis(spread_orders, jnp.minimum(position, TOK_DEV - 1), axis=3)
    send_table = jnp.where(filled, picked, -1).astype(jnp.int32)
    arriving = jnp.transpose(filled, (0, 2, 1, 3)).reshape(PACK_COUNT, N_CTX, N_CTX * CAP)
    ranked = jnp.argsort(jnp.where(arriving, 0, 1), axis=2, stable=True)[:, :, :TOK_DEV].astype(jnp.int32)
    shuffle = jax.vmap(lambda subkey: jax.random.permutation(subkey, TOK_DEV))(jax.random.split(key_order, PACK_COUNT * N_CTX))
    shuffle = shuffle.reshape(PACK_COUNT, N_CTX, TOK_DEV).astype(jnp.int32)
    take_table = jnp.take_along_axis(ranked, shuffle, axis=2).reshape(PACK_COUNT, N_CTX * TOK_DEV).astype(jnp.int32)
    return (send_table, take_table)


def draw_send_rows(key, part):
    send_table, take_table = route_tables(key)
    return send_table


def draw_take_slots(key, part):
    send_table, take_table = route_tables(key)
    return take_table


def draw_queries(key, part):
    key = jax.random.fold_in(key, 11)
    shape = (PACK_COUNT, PACK_TOKENS, QUERY_HEADS * HEAD_SIZE)
    values = jnp.clip(jax.random.normal(key, shape, jnp.float32), -5.0, 5.0)
    return values.astype(jnp.bfloat16)


def block_levels(own_key, shape, shards, least, high):
    factor_of = 1.0
    for dim, blocks in shards:
        heights = jax.random.uniform(jax.random.fold_in(jax.random.fold_in(own_key, 6), dim), (blocks,), jnp.float32, least / len(shards), high / len(shards))
        factor_of = factor_of * jnp.repeat(jnp.exp(heights), shape[dim] // blocks).reshape((-1,) + (1,) * (len(shape) - 1 - dim))
    return factor_of


def split_up(count, total, limit, lean):
    loads = [(1 << 20) // math.isqrt(rank ** lean) + 1 for rank in range(2, count + 1)]
    rest, holding = total - limit - (count - 1), [1] * (count - 1)
    while rest > 0:
        free = [i for i in range(count - 1) if holding[i] < limit]
        whole, budget = sum([loads[i] for i in free]), rest
        for i in free:
            more = min(limit - holding[i], max(1, budget * loads[i] // whole), rest)
            holding[i] = holding[i] + more
            rest = rest - more
    return np.array([limit] + holding)


def ragged(rng, amount, total, reach, lean):
    if amount == 2:
        one = jax.random.randint(rng, (), max(1, total - reach), min(reach, total - 1) + 1)
        return jnp.stack([one, total - one])
    tallies = jnp.asarray(split_up(amount, total, reach, lean), jnp.int32)
    twos = (amount - 1) // 2
    giver, receiver = tallies[1:1 + 2 * twos:2], tallies[2:2 + 2 * twos:2]
    margin = jnp.minimum(giver - 1, reach - receiver)
    moved = jax.random.randint(jax.random.fold_in(rng, 1), (twos,), 0, 1 << 20) % (margin + 1)
    tallies = tallies.at[1:1 + 2 * twos:2].set(giver - moved).at[2:2 + 2 * twos:2].set(receiver + moved)
    return tallies[jax.random.permutation(jax.random.fold_in(rng, 2), amount)]


def centred(rng, extent, deviation, bound, cuts=(), held_as=jnp.bfloat16):
    drawn = jax.random.normal(rng, extent, jnp.float32) * deviation
    if len(cuts) > 0:
        drawn = block_levels(rng, extent, cuts, -0.22, 0.18) * drawn
    return jnp.clip(drawn, min=-bound, max=bound).astype(held_as)


def setup_inputs(seed: int = 0) -> dict:
    arg_keys = jax.random.split(jax.random.key(seed), 7)
    return {
        "queries": draw_queries(jax.random.fold_in(arg_keys[6], 71), 0),
        "packed_keys_values": centred(arg_keys[1], (PACK_COUNT, PACK_TOKENS, 2 * KEY_VALUE_HEADS * HEAD_SIZE), 1.0, 5.0, ((0, 8), (1, 32))),
        "cotangents": centred(arg_keys[2], (PACK_COUNT, PACK_TOKENS, 2, QUERY_HEADS * HEAD_SIZE), 1.0, 5.0, ((0, 8), (1, 32))),
        "send_rows": draw_send_rows(jax.random.fold_in(arg_keys[6], 71), 0),
        "take_slots": draw_take_slots(jax.random.fold_in(arg_keys[6], 71), 0),
        "segment_ids": jax.vmap(lambda own: jnp.searchsorted(jnp.cumsum(ragged(own, SEGS, PACK_TOKENS, DOC_MOST, 2)), jnp.arange(PACK_TOKENS), side="right"))(jax.random.split(arg_keys[5], PACK_COUNT)).reshape((PACK_COUNT, PACK_TOKENS)).astype(jnp.int32),
    }


def head_forward(query_rows, key_rows, value_rows, allowed):
    score_scale = 1.0 / math.sqrt(query_rows.shape[-1])
    scores = jnp.dot(query_rows, key_rows.T, preferred_element_type=jnp.float32) * score_scale
    masked = jnp.where(allowed, scores, -1e+30)
    row_top = lax.optimization_barrier(jnp.max(masked, axis=1, keepdims=True))
    weights = jnp.where(allowed, jnp.exp(masked - row_top), 0.0)
    probabilities = weights / lax.optimization_barrier(jnp.sum(weights, axis=1, keepdims=True))
    blended_rows = jnp.dot(probabilities.astype(jnp.bfloat16), value_rows, preferred_element_type=jnp.float32)
    return (blended_rows, probabilities)

def head_backward(upstream_rows, probabilities, blended_rows, key_rows, value_rows, group_width):
    score_scale = 1.0 / math.sqrt(key_rows.shape[-1])
    bias_grads = []
    for probe_index in range(2):
        upstream = upstream_rows[probe_index]
        row_delta = lax.optimization_barrier(jnp.sum(upstream.astype(jnp.float32) * blended_rows, axis=1, keepdims=True))
        prob_grad = jnp.dot(upstream, value_rows.T, preferred_element_type=jnp.float32)
        score_grad = probabilities * (prob_grad - row_delta)
        column_sums = lax.optimization_barrier(jnp.sum(score_grad.reshape(group_width, -1, score_grad.shape[1]), axis=1))
        bias_grads.append(jnp.dot(column_sums, key_rows.astype(jnp.float32), precision=lax.Precision.HIGHEST) * score_scale)
    return jnp.stack(bias_grads)

def attend_block(query_tile_block, key_value_block, upstream_gradient_block, allowed):
    row_total = query_tile_block.shape[0]
    group_width = QUERY_HEADS // KEY_VALUE_HEADS
    query_head_rows = query_tile_block.reshape(row_total, KEY_VALUE_HEADS, group_width, HEAD_SIZE).transpose(1, 2, 0, 3).reshape(KEY_VALUE_HEADS, group_width * row_total, HEAD_SIZE)
    key_head_rows = key_value_block[:, :KEY_VALUE_HEADS * HEAD_SIZE].reshape(-1, KEY_VALUE_HEADS, HEAD_SIZE).transpose(1, 0, 2)
    value_head_rows = key_value_block[:, KEY_VALUE_HEADS * HEAD_SIZE:].reshape(-1, KEY_VALUE_HEADS, HEAD_SIZE).transpose(1, 0, 2)
    upstream_head_rows = upstream_gradient_block.reshape(row_total, 2, KEY_VALUE_HEADS, group_width, HEAD_SIZE).transpose(2, 1, 3, 0, 4).reshape(KEY_VALUE_HEADS, 2, group_width * row_total, HEAD_SIZE)
    tiled_mask = jnp.tile(allowed, (group_width, 1))
    blended_rows, probabilities = jax.vmap(head_forward, in_axes=(0, 0, 0, None))(query_head_rows, key_head_rows, value_head_rows, tiled_mask)
    backward = partial(head_backward, group_width=group_width)
    bias_grads = jax.vmap(backward)(upstream_head_rows, probabilities, blended_rows, key_head_rows, value_head_rows)
    attended_rows = blended_rows.reshape(KEY_VALUE_HEADS, group_width, row_total, HEAD_SIZE).transpose(2, 0, 1, 3).reshape(row_total, QUERY_HEADS * HEAD_SIZE)
    return (attended_rows.astype(jnp.bfloat16), bias_grads.transpose(1, 0, 2, 3).reshape(2, QUERY_HEADS * HEAD_SIZE))

def pack_result(operands):
    pack_queries, pack_pairs, pack_upstream, pack_send, pack_take, pack_segments = operands
    source = pack_take // CAP
    slot_number = pack_take % CAP
    owner_device = jnp.arange(PACK_TOKENS, dtype=jnp.int32) // TOK_DEV
    local_rows = pack_send[source, owner_device, slot_number]
    packing_rows = source * TOK_DEV + local_rows
    owner_queries = pack_queries[packing_rows]
    owner_pairs = pack_pairs[packing_rows]
    owner_upstream = pack_upstream[packing_rows]
    padding = (GROUP_MOST - 1) * TOK_DEV
    padded_pairs = jnp.concatenate([jnp.zeros((padding, owner_pairs.shape[1]), owner_pairs.dtype), owner_pairs], axis=0)
    padded_segments = jnp.concatenate([jnp.full((padding,), -1, jnp.int32), pack_segments.astype(jnp.int32)], axis=0)
    relative = jnp.arange(GROUP_MOST * TOK_DEV, dtype=jnp.int32) - padding
    query_index = jnp.arange(TOK_DEV, dtype=jnp.int32)

    def block_result(block_index):
        first_row = (block_index * TOK_DEV).astype(jnp.int32)
        query_tile_block = lax.dynamic_slice_in_dim(owner_queries, first_row, TOK_DEV, 0)
        upstream_gradient_block = lax.dynamic_slice_in_dim(owner_upstream, first_row, TOK_DEV, 0)
        segment_query = lax.dynamic_slice_in_dim(pack_segments.astype(jnp.int32), first_row, TOK_DEV, 0)
        key_value_block = lax.dynamic_slice_in_dim(padded_pairs, first_row, GROUP_MOST * TOK_DEV, 0)
        segment_key = lax.dynamic_slice_in_dim(padded_segments, first_row, GROUP_MOST * TOK_DEV, 0)
        allowed = (segment_query[:, None] == segment_key[None, :]) & (relative[None, :] <= query_index[:, None])
        return attend_block(query_tile_block, key_value_block, upstream_gradient_block, allowed)
    outputs, grad_blocks = lax.map(block_result, jnp.arange(N_CTX, dtype=jnp.int32))
    return (outputs.reshape(PACK_TOKENS, QUERY_HEADS * HEAD_SIZE), lax.optimization_barrier(jnp.sum(grad_blocks, axis=0)))

def reference(queries, packed_keys_values, cotangents, send_rows, take_slots, segment_ids):
    attention_out, pack_grads = lax.map(pack_result, (queries, packed_keys_values, cotangents, send_rows, take_slots, segment_ids))
    totals = lax.optimization_barrier(jnp.sum(pack_grads, axis=0))
    bias_curvature = (totals[0] * totals[0] + totals[1] * totals[1]) / (2.0 * PACK_COUNT * PACK_TOKENS)
    return (attention_out, bias_curvature)
```

```python
import functools
import math

import jax
import jax.numpy as jnp
from jax import lax
from jax.experimental import pallas as pl
from jax.experimental.pallas import tpu as pltpu
from jax.sharding import PartitionSpec as P

QUERY_HEADS = 40
KEY_VALUE_HEADS = 8
HEAD_SIZE = 128
TOK = 192
CAP = 7
OWNERS = 32
RING = 4
GROUP = QUERY_HEADS // KEY_VALUE_HEADS
KV_LOCAL = KEY_VALUE_HEADS // RING
Q_COLS = QUERY_HEADS * HEAD_SIZE // RING
K_COLS = KV_LOCAL * HEAD_SIZE
SLOTS = 8 * RING
WINDOW = 4 * TOK
BEHIND = 3 * TOK
VMEM = 60 * 1024 * 1024
MESH = pl.DeviceIdType.MESH
F32 = jnp.float32
BF16 = jnp.bfloat16


def peer(ctx):
    return (lax.axis_index("dp"), ctx)


def spread_kernel(q, kv, cot, meta, qx, cx, kvall, metaall,
                  loc_sem, kvs, kvr, qs, qr, cs, cr, ms, mr, zs, zr, ys, yr, yzs, yzr):
    me = lax.axis_index("ctx")
    x = lax.rem(me, RING)
    base = me - x
    zoff = lax.rem(me // 4, 2)
    zpeer = me + 4 - 8 * zoff
    zbase = zpeer - x
    y = me // 8

    barrier = pltpu.get_barrier_semaphore()

    @pl.loop(1, OWNERS)
    def _(d):
        pl.semaphore_signal(barrier, inc=1, device_id=peer(lax.rem(me + d, OWNERS)), device_id_type=MESH)

    local = [
        pltpu.make_async_copy(kv.at[:, pl.ds(x * K_COLS, K_COLS)], kvall.at[me, :, pl.ds(0, K_COLS)], loc_sem.at[0]),
        pltpu.make_async_copy(
            kv.at[:, pl.ds((RING + x) * K_COLS, K_COLS)], kvall.at[me, :, pl.ds(K_COLS, K_COLS)], loc_sem.at[1]),
        pltpu.make_async_copy(q.at[:, pl.ds(x * Q_COLS, Q_COLS)], qx.at[x], loc_sem.at[2]),
        pltpu.make_async_copy(cot.at[:, :, pl.ds(x * Q_COLS, Q_COLS)], cx.at[x], loc_sem.at[3]),
        pltpu.make_async_copy(meta, metaall.at[me], loc_sem.at[4]),
    ]
    for copy in local:
        copy.start()
    pl.semaphore_wait(barrier, OWNERS - 1)

    def kv_copy(d, half, to):
        g = lax.rem(x + d, RING)
        return pltpu.make_async_remote_copy(
            kv.at[:, pl.ds((half * RING + g) * K_COLS, K_COLS)],
            kvall.at[to, :, pl.ds(half * K_COLS, K_COLS)],
            kvs.at[d, half], kvr.at[d, half], device_id=peer(base + g), device_id_type=MESH)

    def q_copy(d, to):
        g = lax.rem(x + d, RING)
        return pltpu.make_async_remote_copy(
            q.at[:, pl.ds(g * Q_COLS, Q_COLS)], qx.at[to], qs.at[d], qr.at[d],
            device_id=peer(base + g), device_id_type=MESH)

    def c_copy(d, to):
        g = lax.rem(x + d, RING)
        return pltpu.make_async_remote_copy(
            cot.at[:, :, pl.ds(g * Q_COLS, Q_COLS)], cx.at[to], cs.at[d], cr.at[d],
            device_id=peer(base + g), device_id_type=MESH)

    def meta_copy(d, to):
        return pltpu.make_async_remote_copy(
            meta, metaall.at[to], ms.at[d], mr.at[d], device_id=peer(lax.rem(me + d, OWNERS)), device_id_type=MESH)

    def z_copy(i, first):
        return pltpu.make_async_remote_copy(
            kvall.at[first + i], kvall.at[first + i], zs.at[i], zr.at[i], device_id=peer(zpeer), device_id_type=MESH)

    def y_copy(d, first):
        return pltpu.make_async_remote_copy(
            kvall.at[pl.ds(first, RING)], kvall.at[pl.ds(first, RING)], ys.at[d], yr.at[d],
            device_id=peer(lax.rem(me + 8 * d, OWNERS)), device_id_type=MESH)

    def yz_copy(d, i, first):
        return pltpu.make_async_remote_copy(
            kvall.at[first + i], kvall.at[first + i], yzs.at[d, i], yzr.at[d, i],
            device_id=peer(lax.rem(me + 8 * d, OWNERS)), device_id_type=MESH)

    def behind(d):
        return base + lax.rem(x + RING - d, RING)

    def y_base(first, d):
        return lax.rem(first + OWNERS - 8 * d, OWNERS)

    for d in (1, 3, 2):
        for half in range(2):
            kv_copy(d, half, me).start()

    @pl.loop(1, OWNERS)
    def _(d):
        meta_copy(d, me).start()

    local[0].wait()
    local[1].wait()
    for d in (1, 3, 2):
        for half in range(2):
            kv_copy(d, half, behind(d)).wait_recv()
    for i in range(RING):
        z_copy(i, base).start()
    for d in (1, 3, 2):
        y_copy(d, base).start()
    for d in (1, 3, 2):
        q_copy(d, x).start()
    for d in (1, 3, 2):
        c_copy(d, x).start()
    for i in range(RING):
        z_copy(i, zbase).wait_recv()
        for d in (1, 3, 2):
            yz_copy(d, i, zbase).start()
    for copy in local[2:]:
        copy.wait()
    for d in (1, 3, 2):
        q_copy(d, lax.rem(x + RING - d, RING)).wait_recv()
    for d in (1, 3, 2):
        c_copy(d, lax.rem(x + RING - d, RING)).wait_recv()
    for d in (1, 3, 2):
        y_copy(d, y_base(base, d)).wait_recv()
        for i in range(RING):
            yz_copy(d, i, y_base(zbase, d)).wait_recv()

    @pl.loop(1, OWNERS)
    def _(d):
        meta_copy(d, lax.rem(me + OWNERS - d, OWNERS)).wait_recv()
        meta_copy(d, me).wait_send()

    for d in (1, 3, 2):
        for half in range(2):
            kv_copy(d, half, me).wait_send()
        q_copy(d, x).wait_send()
        c_copy(d, x).wait_send()
        y_copy(d, base).wait_send()
        for i in range(RING):
            yz_copy(d, i, zbase).wait_send()
    for i in range(RING):
        z_copy(i, base).wait_send()


def spread(q, kv, cot, meta):
    hbm = pl.BlockSpec(memory_space=pl.ANY)
    dma = pltpu.SemaphoreType.DMA
    return pl.pallas_call(
        spread_kernel,
        out_shape=(
            jax.ShapeDtypeStruct((RING, TOK, Q_COLS), BF16),
            jax.ShapeDtypeStruct((RING, 2, TOK, Q_COLS), BF16),
            jax.ShapeDtypeStruct((OWNERS, TOK, 2 * K_COLS), BF16),
            jax.ShapeDtypeStruct((OWNERS, 8, 256), jnp.int32),
        ),
        in_specs=[hbm] * 4,
        out_specs=(hbm,) * 4,
        scratch_shapes=[
            dma((5,)), dma((RING, 2)), dma((RING, 2)), dma((RING,)), dma((RING,)), dma((RING,)), dma((RING,)),
            dma((OWNERS,)), dma((OWNERS,)), dma((RING,)), dma((RING,)), dma((RING,)), dma((RING,)),
            dma((RING, RING)), dma((RING, RING)),
        ],
        compiler_params=pltpu.CompilerParams(collective_id=0, has_side_effects=True),
        name="spread",
    )(q, kv, cot, meta)


def turned_dot(a, b):
    return lax.dot_general(a, b, (((0,), (0,)), ((), ())), preferred_element_type=F32)


def dot_t(a, b):
    return lax.dot_general(a, b, (((1,), (1,)), ((), ())), preferred_element_type=F32)


def attend_kernel(kind, sbase, q, c, kv, rows, codes, segs, keysegs, out, grads,
                  qslots, cslots, kvslots, kvs, acc):
    row_iota = lax.broadcasted_iota(jnp.int32, (TOK, 256), 0)

    def one_hot(row):
        return jnp.where(row_iota == row, 1.0, 0.0).astype(BF16)

    first = sbase[0]

    def ring_rows(i, carry):
        del carry
        hots = [one_hot(rows[pl.ds(first + 2 * i + j, 1), :]) for j in range(2)]

        def put(ref, parts):
            both = jnp.concatenate([part.reshape(OWNERS, 8, Q_COLS) for part in parts], axis=1)
            ref[:, pl.ds(pl.multiple_of(16 * i, 16), 16), :] = both.astype(BF16)

        put(qslots, [turned_dot(hots[j], q[2 * i + j]) for j in range(2)])
        for p in range(2):
            put(cslots.at[p], [turned_dot(hots[j], c[2 * i + j, p]) for j in range(2)])
        return 0

    lax.fori_loop(0, 2, ring_rows, 0)

    def source_rows(i, carry):
        del carry
        parts = [
            turned_dot(one_hot(rows[pl.ds(2 * i + j, 1), :]), kv[2 * i + j]).reshape(OWNERS, 8, 2 * K_COLS)
            for j in range(2)
        ]
        kvslots[:, pl.ds(pl.multiple_of(16 * i, 16), 16), :] = jnp.concatenate(parts, axis=1).astype(BF16)
        return 0

    lax.fori_loop(0, OWNERS // 2, source_rows, 0)

    acc[...] = jnp.zeros_like(acc)
    kvs[pl.ds(0, BEHIND), :] = jnp.zeros((BEHIND, 2 * K_COLS), BF16)
    code_iota = lax.broadcasted_iota(jnp.int32, (256, TOK), 0)
    slot_code = lax.broadcasted_iota(jnp.int32, (SLOTS, TOK), 0) + first * 8
    own_row = lax.broadcasted_iota(jnp.int32, (SLOTS, TOK), 1)
    scale = 1.0 / math.sqrt(HEAD_SIZE)
    exponent = scale * math.log2(math.e)

    def owner(t, carry):
        del carry
        code = codes[pl.ds(t, 1), :]
        hot = jnp.where(code_iota == code, 1.0, 0.0).astype(BF16)
        kvs[pl.ds(pl.multiple_of(BEHIND + t * TOK, 64), TOK), :] = turned_dot(hot, kvslots[t]).astype(BF16)
        mine = slot_code == code
        row_at = jnp.sum(jnp.where(mine, (own_row + BEHIND).astype(F32), 0.0), axis=1, keepdims=True)
        row_seg = jnp.sum(jnp.where(mine, (segs[pl.ds(t, 1), :] + 1).astype(F32), 0.0), axis=1, keepdims=True) - 1.0

        def attend(width):
            start = pl.multiple_of(BEHIND + (t + 1) * TOK - width, 64)
            key_at = lax.broadcasted_iota(jnp.int32, (SLOTS, width), 1).astype(F32) + float(WINDOW - width)
            key_seg = keysegs[pl.ds(t, 1), WINDOW - width:].astype(F32)
            bias = jnp.where((key_at <= row_at) & (key_seg == row_seg), 0.0, -1e30)
            for a in range(KV_LOCAL):
                cols = a * GROUP * HEAD_SIZE

                def heads(ref):
                    return jnp.concatenate(
                        [ref[t, :, cols + h * HEAD_SIZE: cols + (h + 1) * HEAD_SIZE] for h in range(GROUP)], axis=0)

                keys = kvs[pl.ds(start, width), a * HEAD_SIZE: (a + 1) * HEAD_SIZE]
                values = kvs[pl.ds(start, width), K_COLS + a * HEAD_SIZE: K_COLS + (a + 1) * HEAD_SIZE]
                scores = dot_t(heads(qslots), keys).reshape(GROUP, SLOTS, width) + bias[None]
                top = jnp.max(scores, axis=2, keepdims=True)
                weights = jnp.exp2((scores - top) * exponent)
                probs = weights * (1.0 / jnp.sum(weights, axis=2, keepdims=True))
                mixed = jnp.dot(
                    probs.astype(BF16).reshape(GROUP * SLOTS, width), values, preferred_element_type=F32)
                for h in range(GROUP):
                    out[t, :, cols + h * HEAD_SIZE: cols + (h + 1) * HEAD_SIZE] = (
                        mixed[h * SLOTS: (h + 1) * SLOTS].astype(BF16))
                sums = []
                for p in range(2):
                    up = heads(cslots.at[p])
                    delta = jnp.sum(up.astype(F32) * mixed, axis=1, keepdims=True)
                    prob_grad = dot_t(up, values)
                    grad = probs * (prob_grad - delta).reshape(GROUP, SLOTS, width)
                    sums.append(jnp.sum(grad.reshape(GROUP, SLOTS // 8, 8, width), axis=1).reshape(GROUP * 8, width))
                sums = jnp.concatenate(sums, axis=0)
                high = sums.astype(BF16)
                low = (sums - high.astype(F32)).astype(BF16)
                both = jnp.concatenate([high, low], axis=0)
                acc[a] += jnp.dot(both, keys, preferred_element_type=F32)

        for n, width in enumerate((256, 384, 512, 768)):
            pl.when(kind[t] == n)(functools.partial(attend, width))
        return 0

    lax.fori_loop(0, OWNERS, owner, 0)

    grads[...] = jnp.zeros_like(grads)
    for p in range(2):
        for a in range(KV_LOCAL):
            total = acc[a, pl.ds(p * GROUP * 8, GROUP * 8), :] + acc[a, pl.ds((2 + p) * GROUP * 8, GROUP * 8), :]
            for h in range(GROUP):
                row = jnp.sum(total[h * 8: (h + 1) * 8], axis=0, keepdims=True) * scale
                grads[pl.ds(p * 16 + a * GROUP + h, 1), :] = row


def attend(kind, sbase, q, c, kv, rows, codes, segs, keysegs):
    vmem = pl.BlockSpec(memory_space=pltpu.VMEM)
    smem = pl.BlockSpec(memory_space=pltpu.SMEM)
    return pl.pallas_call(
        attend_kernel,
        out_shape=(
            jax.ShapeDtypeStruct((OWNERS, SLOTS, Q_COLS), BF16),
            jax.ShapeDtypeStruct((32, HEAD_SIZE), F32),
        ),
        in_specs=[smem, smem] + [vmem] * 7,
        out_specs=(vmem, vmem),
        scratch_shapes=[
            pltpu.VMEM((OWNERS, SLOTS, Q_COLS), BF16),
            pltpu.VMEM((2, OWNERS, SLOTS, Q_COLS), BF16),
            pltpu.VMEM((OWNERS, 256, 2 * K_COLS), BF16),
            pltpu.VMEM((BEHIND + OWNERS * TOK, 2 * K_COLS), BF16),
            pltpu.VMEM((KV_LOCAL, 4 * GROUP * 8, HEAD_SIZE), F32),
        ],
        compiler_params=pltpu.CompilerParams(vmem_limit_bytes=VMEM),
        name="attend",
    )(kind, sbase, q, c, kv, rows, codes, segs, keysegs)


def collect_kernel(token_total, slots, grads, owned, curve,
                   parts, yparts, squares, loc_sem, os, orr, gs, gr, ys, yr, xs, xr):
    me = lax.axis_index("ctx")
    dp = lax.axis_index("dp")
    x = lax.rem(me, RING)
    base = me - x
    yz = me // RING
    zoff = lax.rem(yz, 2)
    line = zoff * 8 + dp

    def line_peer(d):
        n = lax.rem(line + d, 16)
        return (lax.rem(n, 8), me + 4 * (n // 8 - zoff))

    barrier = pltpu.get_barrier_semaphore()

    @pl.loop(1, OWNERS)
    def _(d):
        pl.semaphore_signal(barrier, inc=1, device_id=peer(lax.rem(me + d, OWNERS)), device_id_type=MESH)

    @pl.loop(1, 16)
    def _(d):
        pl.semaphore_signal(barrier, inc=1, device_id=line_peer(d), device_id_type=MESH)

    parts[pl.ds(line, 1)] = grads[...][None]
    own = pltpu.make_async_copy(slots.at[me], owned.at[yz, :, pl.ds(x * Q_COLS, Q_COLS)], loc_sem)
    own.start()
    pl.semaphore_wait(barrier, OWNERS - 1 + 15)

    def g_copy(d, at):
        return pltpu.make_async_remote_copy(
            parts.at[at], parts.at[at], gs.at[d], gr.at[d], device_id=line_peer(d), device_id_type=MESH)

    @pl.loop(1, 16)
    def _(d):
        g_copy(d, line).start()

    def o_copy(d, target, source):
        return pltpu.make_async_remote_copy(
            slots.at[target],
            owned.at[source // RING, :, pl.ds(pl.multiple_of(lax.rem(source, RING) * Q_COLS, Q_COLS), Q_COLS)],
            os.at[d], orr.at[d], device_id=peer(target), device_id_type=MESH)

    @pl.loop(1, OWNERS)
    def _(d):
        o_copy(d, lax.rem(me + d, OWNERS), me).start()

    @pl.loop(1, 16)
    def _(d):
        g_copy(d, lax.rem(line + 16 - d, 16)).wait_recv()
        g_copy(d, line).wait_send()

    y = me // 8
    yparts[pl.ds(y, 1)] = jnp.sum(parts[...], axis=0)[None]

    def y_copy(d, at):
        return pltpu.make_async_remote_copy(
            yparts.at[at], yparts.at[at], ys.at[d], yr.at[d],
            device_id=peer(lax.rem(me + 8 * d, OWNERS)), device_id_type=MESH)

    for d in range(1, RING):
        y_copy(d, y).start()
    for d in range(1, RING):
        y_copy(d, lax.rem(y + RING - d, RING)).wait_recv()
        y_copy(d, y).wait_send()
    total = jnp.sum(yparts[...], axis=0)
    squares[pl.ds(x, 1)] = ((total[:16] * total[:16] + total[16:] * total[16:]) / token_total)[None]

    def x_copy(d, at):
        return pltpu.make_async_remote_copy(
            squares.at[at], squares.at[at], xs.at[d], xr.at[d],
            device_id=peer(base + lax.rem(x + d, RING)), device_id_type=MESH)

    for d in range(1, RING):
        x_copy(d, x).start()
    for d in range(1, RING):
        x_copy(d, lax.rem(x + RING - d, RING)).wait_recv()
        x_copy(d, x).wait_send()
    curve[...] = squares[...]

    own.wait()

    @pl.loop(1, OWNERS)
    def _(d):
        o_copy(d, me, lax.rem(me + OWNERS - d, OWNERS)).wait_recv()
        o_copy(d, lax.rem(me + d, OWNERS), me).wait_send()


def collect(slots, grads, token_total):
    hbm = pl.BlockSpec(memory_space=pl.ANY)
    vmem = pl.BlockSpec(memory_space=pltpu.VMEM)
    dma = pltpu.SemaphoreType.DMA
    return pl.pallas_call(
        functools.partial(collect_kernel, token_total),
        out_shape=(
            jax.ShapeDtypeStruct((OWNERS // RING, SLOTS, RING * Q_COLS), BF16),
            jax.ShapeDtypeStruct((RING, 16, HEAD_SIZE), F32),
        ),
        in_specs=[hbm, vmem],
        out_specs=(hbm, vmem),
        scratch_shapes=[
            pltpu.VMEM((16, 32, HEAD_SIZE), F32),
            pltpu.VMEM((RING, 32, HEAD_SIZE), F32),
            pltpu.VMEM((RING, 16, HEAD_SIZE), F32),
            dma, dma((OWNERS,)), dma((OWNERS,)), dma((16,)), dma((16,)),
            dma((RING,)), dma((RING,)), dma((RING,)), dma((RING,)),
        ],
        compiler_params=pltpu.CompilerParams(collective_id=1, has_side_effects=True),
        name="collect",
    )(slots, grads)


def order_kernel(code, slots, out):
    iota = lax.broadcasted_iota(jnp.int32, (256, TOK), 0)
    hot = jnp.where(iota == code[...], 1.0, 0.0).astype(BF16)
    out[...] = turned_dot(hot, slots[...]).astype(BF16)


def order(code, slots):
    return pl.pallas_call(
        order_kernel,
        grid=(RING,),
        out_shape=jax.ShapeDtypeStruct((TOK, RING * Q_COLS), BF16),
        in_specs=[
            pl.BlockSpec((1, TOK), lambda i: (0, 0)),
            pl.BlockSpec((256, Q_COLS), lambda i: (0, i)),
        ],
        out_specs=pl.BlockSpec((TOK, Q_COLS), lambda i: (0, i)),
        name="order",
    )(code, slots)


def per_device(queries, packed_keys_values, cotangents, send_rows, take_slots, segment_ids):
    me = lax.axis_index("ctx")
    code = take_slots + take_slots // CAP
    meta = jnp.concatenate([
        jnp.pad(code, ((0, 0), (0, 256 - TOK))),
        jnp.pad(segment_ids, ((0, 0), (0, 256 - TOK))),
        jnp.pad(send_rows[0, 0], ((0, 0), (0, 8 - CAP)), constant_values=-1).reshape(1, 256),
        jnp.zeros((5, 256), jnp.int32),
    ], axis=0)
    cot = jnp.transpose(cotangents[0], (1, 0, 2))
    qx, cx, kvall, metaall = spread(queries[0], packed_keys_values[0], cot, meta)
    codes = metaall[:, 0, :TOK]
    segs = metaall[:, 1, :TOK]
    rows = metaall[:, 2, :]
    flat = jnp.concatenate([jnp.full((BEHIND,), -2, jnp.int32), segs.reshape(-1)])
    keysegs = jnp.concatenate([flat[i * TOK: i * TOK + OWNERS * TOK].reshape(OWNERS, TOK) for i in range(4)], axis=1)
    starts = jnp.sum(segs.reshape(1, -1) < segs[:, :1], axis=1)
    need = (jnp.arange(OWNERS) + 1) * TOK - starts
    kind = (need > 256).astype(jnp.int32) + (need > 384) + (need > 512)
    sbase = (me - lax.rem(me, RING)).reshape(1)
    slots, grads = attend(kind.astype(jnp.int32), sbase, qx, cx, kvall, rows, codes, segs, keysegs)
    token_total = 2.0 * TOK * OWNERS * lax.axis_size("dp")
    owned, curve = collect(slots, grads, token_total)
    out = order(code, owned.reshape(256, RING * Q_COLS))
    return out[None], curve[:, : QUERY_HEADS // RING].reshape(-1)


def solution(mesh):
    placed = (
        P("dp", "ctx", None),
        P("dp", "ctx", None),
        P("dp", "ctx", None, None),
        P("dp", "ctx", None, None),
        P("dp", "ctx"),
        P("dp", "ctx"),
    )
    return jax.shard_map(
        per_device,
        mesh=mesh,
        in_specs=placed,
        out_specs=(P("dp", "ctx", None), P()),
        check_vma=False,
    )
```

```python
import functools
import math

import jax
import jax.numpy as jnp
from jax import lax
from jax.experimental import pallas as pl
from jax.experimental.pallas import tpu as pltpu
from jax.sharding import PartitionSpec as P

QUERY_HEADS = 40
KEY_VALUE_HEADS = 8
HEAD_SIZE = 128
TOK = 192
CAP = 7
OWNERS = 32
RING = 4
GROUP = QUERY_HEADS // KEY_VALUE_HEADS
KV_LOCAL = KEY_VALUE_HEADS // RING
Q_COLS = QUERY_HEADS * HEAD_SIZE // RING
A_COLS = GROUP * HEAD_SIZE
K_COLS = KV_LOCAL * HEAD_SIZE
SLOTS = 8 * RING
WINDOW = 4 * TOK
BEHIND = 3 * TOK
LINE = 16
VMEM = 60 * 1024 * 1024
MESH = pl.DeviceIdType.MESH
F32 = jnp.float32
BF16 = jnp.bfloat16


def turned_dot(a, b):
    return lax.dot_general(a, b, (((0,), (0,)), ((), ())), preferred_element_type=F32)


def dot_t(a, b):
    return lax.dot_general(a, b, (((1,), (1,)), ((), ())), preferred_element_type=F32)


def one_hot(row, count):
    iota = lax.broadcasted_iota(jnp.int32, (count, row.shape[1]), 0)
    return jnp.where(iota == row, 1.0, 0.0).astype(BF16)


def peer(ctx):
    return (lax.axis_index("dp"), ctx)


def kernel(token_total, q, kv, cot, meta, result, curve,
           qbuf, cbuf, kvbuf, metaall, qslots, cslots, kvslots, kvs, bias, slots, owned, acc, grads,
           parts, yparts, squares,
           loc, kvsend, kvrecv, qsend, qrecv, csend, crecv, msend, mrecv, zsend, zrecv, ysend, yrecv, yzsend, yzrecv,
           osend, orecv, gsend, grecv, bsend, brecv, xsend, xrecv):
    me = lax.axis_index("ctx")
    dp = lax.axis_index("dp")
    x = lax.rem(me, RING)
    base = me - x
    yz = me // RING
    zoff = lax.rem(yz, 2)
    y = me // 8
    zpeer = me + 4 - 8 * zoff
    zbase = zpeer - x
    line = zoff * 8 + dp
    directions = (1, 3, 2)
    scale = 1.0 / math.sqrt(HEAD_SIZE)
    exponent = scale * math.log2(math.e)

    def line_peer(d):
        n = lax.rem(line + d, LINE)
        return (lax.rem(n, 8), me + 4 * (n // 8 - zoff))

    def up(d):
        return lax.rem(x + d, RING)

    def down(d):
        return lax.rem(x + RING - d, RING)

    def y_base(first, d):
        return lax.rem(first + OWNERS - 8 * d, OWNERS)

    def kv_copy(a, d, half, to):
        return pltpu.make_async_remote_copy(
            kv.at[:, pl.ds((half * RING + up(d)) * K_COLS + a * HEAD_SIZE, HEAD_SIZE)],
            kvbuf.at[a, to, :, pl.ds(half * HEAD_SIZE, HEAD_SIZE)],
            kvsend.at[a, d, half], kvrecv.at[a, d, half], device_id=peer(base + up(d)), device_id_type=MESH)

    def q_copy(a, d, to):
        return pltpu.make_async_remote_copy(
            q.at[:, pl.ds(up(d) * Q_COLS + a * A_COLS, A_COLS)], qbuf.at[a, to], qsend.at[a, d], qrecv.at[a, d],
            device_id=peer(base + up(d)), device_id_type=MESH)

    def c_copy(a, d, to):
        return pltpu.make_async_remote_copy(
            cot.at[:, :, pl.ds(up(d) * Q_COLS + a * A_COLS, A_COLS)], cbuf.at[a, to], csend.at[a, d], crecv.at[a, d],
            device_id=peer(base + up(d)), device_id_type=MESH)

    def meta_copy(d, to):
        return pltpu.make_async_remote_copy(
            meta, metaall.at[3 + to], msend.at[d], mrecv.at[d],
            device_id=peer(lax.rem(me + d, OWNERS)), device_id_type=MESH)

    def z_copy(a, i, first):
        return pltpu.make_async_remote_copy(
            kvbuf.at[a, first + i], kvbuf.at[a, first + i], zsend.at[a, i], zrecv.at[a, i],
            device_id=peer(zpeer), device_id_type=MESH)

    def y_copy(a, d, first):
        return pltpu.make_async_remote_copy(
            kvbuf.at[a, pl.ds(first, RING)], kvbuf.at[a, pl.ds(first, RING)], ysend.at[a, d], yrecv.at[a, d],
            device_id=peer(lax.rem(me + 8 * d, OWNERS)), device_id_type=MESH)

    def yz_copy(a, d, i, first):
        return pltpu.make_async_remote_copy(
            kvbuf.at[a, first + i], kvbuf.at[a, first + i], yzsend.at[a, d, i], yzrecv.at[a, d, i],
            device_id=peer(lax.rem(me + 8 * d, OWNERS)), device_id_type=MESH)

    def o_copy(a, d, target, source):
        return pltpu.make_async_remote_copy(
            slots.at[a, target],
            owned.at[source // RING, :, pl.ds(pl.multiple_of(lax.rem(source, RING) * Q_COLS + a * A_COLS, 128), A_COLS)],
            osend.at[a, d], orecv.at[a, d], device_id=peer(target), device_id_type=MESH)

    def kv_local(a, half):
        return pltpu.make_async_copy(
            kv.at[:, pl.ds((half * RING + x) * K_COLS + a * HEAD_SIZE, HEAD_SIZE)],
            kvbuf.at[a, me, :, pl.ds(half * HEAD_SIZE, HEAD_SIZE)], loc.at[a, half])

    def q_local(a):
        return pltpu.make_async_copy(q.at[:, pl.ds(x * Q_COLS + a * A_COLS, A_COLS)], qbuf.at[a, x], loc.at[a, 2])

    def c_local(a):
        return pltpu.make_async_copy(
            cot.at[:, :, pl.ds(x * Q_COLS + a * A_COLS, A_COLS)], cbuf.at[a, x], loc.at[a, 3])

    def o_local(a):
        return pltpu.make_async_copy(
            slots.at[a, me], owned.at[yz, :, pl.ds(pl.multiple_of(x * Q_COLS + a * A_COLS, 128), A_COLS)], loc.at[a, 4])

    meta_local = pltpu.make_async_copy(meta, metaall.at[3 + me], loc.at[0, 5])

    barrier = pltpu.get_barrier_semaphore()

    @pl.loop(1, OWNERS)
    def _(d):
        pl.semaphore_signal(barrier, inc=1, device_id=peer(lax.rem(me + d, OWNERS)), device_id_type=MESH)

    @pl.loop(1, LINE)
    def _(d):
        pl.semaphore_signal(barrier, inc=1, device_id=line_peer(d), device_id_type=MESH)

    meta_local.start()
    for a in range(KV_LOCAL):
        for half in range(2):
            kv_local(a, half).start()
        q_local(a).start()
        c_local(a).start()
    metaall[pl.ds(0, 3)] = jnp.zeros((3, 8, 256), jnp.int32)
    acc[...] = jnp.zeros_like(acc)
    for a in range(KV_LOCAL):
        kvs[a, pl.ds(0, BEHIND), :] = jnp.zeros((BEHIND, 2 * HEAD_SIZE), BF16)
    pl.semaphore_wait(barrier, OWNERS - 1 + LINE - 1)

    for a in range(KV_LOCAL):
        for d in directions:
            for half in range(2):
                kv_copy(a, d, half, me).start()

    @pl.loop(1, OWNERS)
    def _(d):
        meta_copy(d, me).start()

    for d in directions:
        q_copy(0, d, x).start()
    for d in directions:
        c_copy(0, d, x).start()

    def pair_rows(a, i):
        parts_ = [
            turned_dot(one_hot(metaall[3 + 2 * i + j][2:3], TOK), kvbuf[a, 2 * i + j])
            .reshape(OWNERS, 8, 2 * HEAD_SIZE) for j in range(2)
        ]
        kvslots[a, :, pl.ds(pl.multiple_of(16 * i, 16), 16), :] = jnp.concatenate(parts_, axis=1).astype(BF16)

    def ring_rows(a, first):
        for i in range(2):
            pair_rows(a, first // 2 + i)

    def ring_into(a, buf, put):
        @pl.loop(0, 2)
        def _(i):
            parts_ = [
                turned_dot(one_hot(metaall[3 + base + 2 * i + j][2:3], TOK), buf(2 * i + j))
                .reshape(OWNERS, 8, A_COLS) for j in range(2)
            ]
            put[:, pl.ds(pl.multiple_of(16 * i, 16), 16), :] = jnp.concatenate(parts_, axis=1).astype(BF16)

    def wait_kv(a):
        for half in range(2):
            kv_local(a, half).wait()
        for d in directions:
            for half in range(2):
                kv_copy(a, d, half, base + down(d)).wait_recv()

    wait_kv(0)
    for i in range(RING):
        z_copy(0, i, base).start()
    for d in directions:
        y_copy(0, d, base).start()
    wait_kv(1)
    for i in range(RING):
        z_copy(1, i, base).start()

    meta_local.wait()

    @pl.loop(1, OWNERS)
    def _(d):
        meta_copy(d, lax.rem(me + OWNERS - d, OWNERS)).wait_recv()

    ring_rows(0, base)

    slot_code = lax.broadcasted_iota(jnp.int32, (SLOTS, TOK), 0) + base * 8
    own_row = lax.broadcasted_iota(jnp.int32, (SLOTS, TOK), 1) + BEHIND
    key_at = lax.broadcasted_iota(jnp.int32, (SLOTS, WINDOW), 1).astype(F32)

    @pl.loop(0, OWNERS)
    def _(t):
        block = metaall[3 + t]
        mine = slot_code == block[0:1, :TOK]
        row_at = jnp.sum(jnp.where(mine, own_row.astype(F32), 0.0), axis=1, keepdims=True)
        row_seg = jnp.sum(jnp.where(mine, block[1:2, :TOK].astype(F32), 0.0), axis=1, keepdims=True)
        key_seg = jnp.zeros((8, WINDOW), jnp.int32)
        for j in range(4):
            wide = jnp.concatenate([metaall[t + j], jnp.zeros((8, WINDOW - 256), jnp.int32)], axis=1)
            key_seg += wide if j == 0 else pltpu.roll(wide, j * TOK, 1)
        allowed = (key_at <= row_at) & (key_seg[1:2].astype(F32) == row_seg)
        bias[t] = jnp.where(allowed, 0.0, -1e30)

    for i in range(RING):
        z_copy(0, i, zbase).wait_recv()
        for d in directions:
            yz_copy(0, d, i, zbase).start()
    for d in directions:
        y_copy(1, d, base).start()
    ring_rows(0, zbase)
    ring_rows(1, base)

    q_local(0).wait()
    for d in directions:
        q_copy(0, d, down(d)).wait_recv()
        q_copy(1, d, x).start()
    ring_into(0, lambda s: qbuf[0, s], qslots)

    for i in range(RING):
        z_copy(1, i, zbase).wait_recv()
        for d in directions:
            yz_copy(1, d, i, zbase).start()
    ring_rows(1, zbase)

    def rest_of_keys(a):
        for d in directions:
            y_copy(a, d, y_base(base, d)).wait_recv()
            ring_rows(a, y_base(base, d))
        for d in directions:
            for i in range(RING):
                yz_copy(a, d, i, y_base(zbase, d)).wait_recv()
            ring_rows(a, y_base(zbase, d))

        @pl.loop(0, OWNERS)
        def _(t):
            hot = one_hot(metaall[3 + t][0:1, :TOK], 256)
            kvs[a, pl.ds(pl.multiple_of(BEHIND + t * TOK, 64), TOK), :] = turned_dot(hot, kvslots[a, t]).astype(BF16)

    def attend(a, d, u):
        t = lax.rem(me + d, OWNERS)
        start = pl.multiple_of(t * TOK, 64)

        def heads(ref):
            return jnp.concatenate([ref[t, :, h * HEAD_SIZE: (h + 1) * HEAD_SIZE] for h in range(GROUP)], axis=0)

        keys = kvs[a, pl.ds(start, WINDOW), :HEAD_SIZE]
        values = kvs[a, pl.ds(start, WINDOW), HEAD_SIZE:]
        scores = dot_t(heads(qslots), keys).reshape(GROUP, SLOTS, WINDOW) + bias[t][None]
        top = jnp.max(scores, axis=2, keepdims=True)
        weights = jnp.exp2((scores - top) * exponent)
        probs = weights * (1.0 / jnp.sum(weights, axis=2, keepdims=True))
        mixed = jnp.dot(probs.astype(BF16).reshape(GROUP * SLOTS, WINDOW), values, preferred_element_type=F32)
        for h in range(GROUP):
            slots[a, t, :, h * HEAD_SIZE: (h + 1) * HEAD_SIZE] = mixed[h * SLOTS: (h + 1) * SLOTS].astype(BF16)
        sums = []
        for p in range(2):
            upstream = heads(cslots.at[p])
            delta = jnp.sum(upstream.astype(F32) * mixed, axis=1, keepdims=True)
            grad = probs * (dot_t(upstream, values) - delta).reshape(GROUP, SLOTS, WINDOW)
            sums.append(jnp.sum(grad.reshape(GROUP, SLOTS // 8, 8, WINDOW), axis=1).reshape(GROUP * 8, WINDOW))
        sums = jnp.concatenate(sums, axis=0)
        high = sums.astype(BF16)
        low = (sums - high.astype(F32)).astype(BF16)
        acc[a, u] += jnp.dot(jnp.concatenate([high, low], axis=0), keys, preferred_element_type=F32)

    def attend_all(a):
        @pl.loop(0, OWNERS // 2)
        def _(i):
            for u in range(2):
                attend(a, 2 * i + u, u)

            @pl.when(i == 0)
            def _():
                o_local(a).start()

            @pl.when(i > 0)
            def _():
                o_copy(a, 2 * i, lax.rem(me + 2 * i, OWNERS), me).start()

            o_copy(a, 2 * i + 1, lax.rem(me + 2 * i + 1, OWNERS), me).start()

    rest_of_keys(0)
    c_local(0).wait()
    for d in directions:
        c_copy(0, d, down(d)).wait_recv()
        c_copy(1, d, x).start()
    for p in range(2):
        ring_into(0, lambda s, p=p: cbuf[0, s, p], cslots.at[p])
    attend_all(0)

    rest_of_keys(1)
    q_local(1).wait()
    for d in directions:
        q_copy(1, d, down(d)).wait_recv()
    ring_into(1, lambda s: qbuf[1, s], qslots)
    c_local(1).wait()
    for d in directions:
        c_copy(1, d, down(d)).wait_recv()
    for p in range(2):
        ring_into(1, lambda s, p=p: cbuf[1, s, p], cslots.at[p])
    attend_all(1)

    grads[...] = jnp.zeros_like(grads)
    for a in range(KV_LOCAL):
        both = acc[a, 0] + acc[a, 1]
        for p in range(2):
            total = both[p * GROUP * 8: (p + 1) * GROUP * 8] + both[(2 + p) * GROUP * 8: (3 + p) * GROUP * 8]
            for h in range(GROUP):
                row = jnp.sum(total[h * 8: (h + 1) * 8], axis=0, keepdims=True) * scale
                grads[pl.ds(p * 16 + a * GROUP + h, 1), :] = row
    parts[pl.ds(line, 1)] = grads[...][None]

    def g_copy(d, at):
        return pltpu.make_async_remote_copy(
            parts.at[at], parts.at[at], gsend.at[d], grecv.at[d], device_id=line_peer(d), device_id_type=MESH)

    @pl.loop(1, LINE)
    def _(d):
        g_copy(d, line).start()

    @pl.loop(1, LINE)
    def _(d):
        g_copy(d, lax.rem(line + LINE - d, LINE)).wait_recv()
        g_copy(d, line).wait_send()

    yparts[pl.ds(y, 1)] = jnp.sum(parts[...], axis=0)[None]

    def b_copy(d, at):
        return pltpu.make_async_remote_copy(
            yparts.at[at], yparts.at[at], bsend.at[d], brecv.at[d],
            device_id=peer(lax.rem(me + 8 * d, OWNERS)), device_id_type=MESH)

    for d in directions:
        b_copy(d, y).start()
    for d in directions:
        b_copy(d, lax.rem(y + RING - d, RING)).wait_recv()
        b_copy(d, y).wait_send()
    total = jnp.sum(yparts[...], axis=0)
    squares[pl.ds(x, 1)] = ((total[:16] * total[:16] + total[16:] * total[16:]) / token_total)[None]

    def x_copy(d, at):
        return pltpu.make_async_remote_copy(
            squares.at[at], squares.at[at], xsend.at[d], xrecv.at[d],
            device_id=peer(base + up(d)), device_id_type=MESH)

    for d in directions:
        x_copy(d, x).start()
    for d in directions:
        x_copy(d, down(d)).wait_recv()
        x_copy(d, x).wait_send()
    curve[...] = squares[...]

    hot = one_hot(metaall[3 + me][0:1, :TOK], 256)
    for a in range(KV_LOCAL):
        o_local(a).wait()

        @pl.loop(1, OWNERS)
        def _(d):
            o_copy(a, d, me, lax.rem(me + OWNERS - d, OWNERS)).wait_recv()

    for i in range(RING):
        cols = pl.ds(i * Q_COLS, Q_COLS)
        result[:, cols] = turned_dot(hot, owned[:, :, cols].reshape(256, Q_COLS)).astype(BF16)

    @pl.loop(1, OWNERS)
    def _(d):
        meta_copy(d, me).wait_send()
        for a in range(KV_LOCAL):
            o_copy(a, d, lax.rem(me + d, OWNERS), me).wait_send()

    for a in range(KV_LOCAL):
        for d in directions:
            for half in range(2):
                kv_copy(a, d, half, me).wait_send()
            q_copy(a, d, x).wait_send()
            c_copy(a, d, x).wait_send()
            y_copy(a, d, base).wait_send()
            for i in range(RING):
                yz_copy(a, d, i, zbase).wait_send()
        for i in range(RING):
            z_copy(a, i, base).wait_send()


def run(q, kv, cot, meta, token_total):
    hbm = pl.BlockSpec(memory_space=pl.ANY)
    vmem = pl.BlockSpec(memory_space=pltpu.VMEM)
    dma = pltpu.SemaphoreType.DMA
    return pl.pallas_call(
        functools.partial(kernel, token_total),
        out_shape=(
            jax.ShapeDtypeStruct((TOK, RING * Q_COLS), BF16),
            jax.ShapeDtypeStruct((RING, 16, HEAD_SIZE), F32),
        ),
        in_specs=[hbm] * 4,
        out_specs=(vmem, vmem),
        scratch_shapes=[
            pltpu.VMEM((KV_LOCAL, RING, TOK, A_COLS), BF16),
            pltpu.VMEM((KV_LOCAL, RING, 2, TOK, A_COLS), BF16),
            pltpu.VMEM((KV_LOCAL, OWNERS, TOK, 2 * HEAD_SIZE), BF16),
            pltpu.VMEM((3 + OWNERS, 8, 256), jnp.int32),
            pltpu.VMEM((OWNERS, SLOTS, A_COLS), BF16),
            pltpu.VMEM((2, OWNERS, SLOTS, A_COLS), BF16),
            pltpu.VMEM((KV_LOCAL, OWNERS, 256, 2 * HEAD_SIZE), BF16),
            pltpu.VMEM((KV_LOCAL, BEHIND + OWNERS * TOK, 2 * HEAD_SIZE), BF16),
            pltpu.VMEM((OWNERS, SLOTS, WINDOW), F32),
            pltpu.VMEM((KV_LOCAL, OWNERS, SLOTS, A_COLS), BF16),
            pltpu.VMEM((OWNERS // RING, SLOTS, RING * Q_COLS), BF16),
            pltpu.VMEM((KV_LOCAL, 2, 4 * GROUP * 8, HEAD_SIZE), F32),
            pltpu.VMEM((32, HEAD_SIZE), F32),
            pltpu.VMEM((LINE, 32, HEAD_SIZE), F32),
            pltpu.VMEM((RING, 32, HEAD_SIZE), F32),
            pltpu.VMEM((RING, 16, HEAD_SIZE), F32),
            dma((KV_LOCAL, 6)),
            dma((KV_LOCAL, RING, 2)), dma((KV_LOCAL, RING, 2)),
            dma((KV_LOCAL, RING)), dma((KV_LOCAL, RING)), dma((KV_LOCAL, RING)), dma((KV_LOCAL, RING)),
            dma((OWNERS,)), dma((OWNERS,)),
            dma((KV_LOCAL, RING)), dma((KV_LOCAL, RING)), dma((KV_LOCAL, RING)), dma((KV_LOCAL, RING)),
            dma((KV_LOCAL, RING, RING)), dma((KV_LOCAL, RING, RING)),
            dma((KV_LOCAL, OWNERS)), dma((KV_LOCAL, OWNERS)),
            dma((LINE,)), dma((LINE,)), dma((RING,)), dma((RING,)), dma((RING,)), dma((RING,)),
        ],
        compiler_params=pltpu.CompilerParams(collective_id=0, has_side_effects=True, vmem_limit_bytes=VMEM),
        name="curvature",
    )(q, kv, cot, meta)


def per_device(queries, packed_keys_values, cotangents, send_rows, take_slots, segment_ids):
    meta = jnp.concatenate([
        jnp.pad(take_slots + take_slots // CAP, ((0, 0), (0, 256 - TOK))),
        jnp.pad(segment_ids + 1, ((0, 0), (0, 256 - TOK))),
        jnp.pad(send_rows[0, 0], ((0, 0), (0, 8 - CAP)), constant_values=-1).reshape(1, 256),
        jnp.zeros((5, 256), jnp.int32),
    ], axis=0)
    cot = jnp.transpose(cotangents[0], (1, 0, 2))
    token_total = 2.0 * TOK * OWNERS * lax.axis_size("dp")
    out, curve = run(queries[0], packed_keys_values[0], cot, meta, token_total)
    return out[None], curve[:, : QUERY_HEADS // RING].reshape(-1)


def solution(mesh):
    placed = (
        P("dp", "ctx", None),
        P("dp", "ctx", None),
        P("dp", "ctx", None, None),
        P("dp", "ctx", None, None),
        P("dp", "ctx"),
        P("dp", "ctx"),
    )
    return jax.shard_map(
        per_device,
        mesh=mesh,
        in_specs=placed,
        out_specs=(P("dp", "ctx", None), P()),
        check_vma=False,
    )
```

```python
import functools
import math

import jax
import jax.numpy as jnp
from jax import lax
from jax.experimental import pallas as pl
from jax.experimental.pallas import tpu as pltpu
from jax.sharding import PartitionSpec as P

QUERY_HEADS = 40
KEY_VALUE_HEADS = 8
HEAD_SIZE = 128
TOK = 192
META = 16
CAP = 7
OWNERS = 32
RING = 4
GROUP = QUERY_HEADS // KEY_VALUE_HEADS
KV_LOCAL = KEY_VALUE_HEADS // RING
Q_COLS = QUERY_HEADS * HEAD_SIZE // RING
K_COLS = KV_LOCAL * HEAD_SIZE
SLOTS = 8 * RING
WINDOW = 4 * TOK
BEHIND = 3 * TOK
LINE = 8
CHUNKS = ((0, 0, 5), (1, 5, 5))
VMEM = 60 * 1024 * 1024
MESH = pl.DeviceIdType.MESH
F32 = jnp.float32
BF16 = jnp.bfloat16


def turned_dot(a, b):
    return lax.dot_general(a, b, (((0,), (0,)), ((), ())), preferred_element_type=F32)


def dot_t(a, b):
    return lax.dot_general(a, b, (((1,), (1,)), ((), ())), preferred_element_type=F32)


def one_hot(row, count):
    iota = lax.broadcasted_iota(jnp.int32, (count, row.shape[1]), 0).astype(F32)
    return jnp.where(iota == row, 1.0, 0.0).astype(BF16)


def kernel(token_total, q, kv, cot, meta, result, curve,
           qbuf, cbuf, kvbuf0, kvbuf1, qslots, cslots, kvslots, kvs, bias, slots, owned, acc, grads,
           parts, yparts, xparts, cparts,
           loc, kvsend, kvrecv, msend, mrecv, qsend, qrecv, csend, crecv, zsend, zrecv, ysend, yrecv, yfsend, yfrecv,
           yzsend, yzrecv, yzfsend, yzfrecv, osend, orecv, gsend, grecv, bsend, brecv, xsend, xrecv, psend, precv):
    kvbuf = (kvbuf0, kvbuf1)
    me = lax.axis_index("ctx")
    dp = lax.axis_index("dp")
    core = lax.rem(dp, 2)
    scale = 1.0 / math.sqrt(HEAD_SIZE)
    exponent = scale * math.log2(math.e)

    def turn(n):
        fast, slow = lax.rem(n, 4), n // 8
        return (slow + core * (fast - slow)) * 8 + lax.rem(n // 4, 2) * 4 + fast + core * (slow - fast)

    here = turn(me)
    x = lax.rem(here, RING)
    base = here - x
    zoff = lax.rem(here // 4, 2)
    y = here // 8
    zhere = here + 4 - 8 * zoff
    zbase = zhere - x
    line = zoff * 4 + dp // 2
    directions = (1, 3, 2)
    ways = (1, 3)

    def peer(place):
        return (dp, turn(place))

    def owner(t):
        return (dp, t)

    def line_peer(d):
        n = lax.rem(line + d, LINE)
        return (lax.rem(n, 4) * 2 + core, me + 4 * (n // 4 - zoff))

    core_peer = (dp + 1 - 2 * core, me)

    def up(d):
        return lax.rem(x + d, RING)

    def down(d):
        return lax.rem(x + RING - d, RING)

    def y_peer(d):
        return peer(lax.rem(here + 8 * d, OWNERS))

    def y_base(first, d):
        return lax.rem(first + OWNERS - 8 * d, OWNERS)

    def forward_way(i):
        return 1 if i < 2 else 3

    def send(src, dst, sems, at, device):
        return pltpu.make_async_remote_copy(
            src, dst, sems[0].at[at], sems[1].at[at], device_id=device, device_id_type=MESH)

    def kv_copy(a, d, half, to):
        return send(
            kv.at[:, pl.ds((half * RING + up(d)) * K_COLS + a * HEAD_SIZE, HEAD_SIZE)],
            kvbuf[a].at[to, pl.ds(0, TOK), pl.ds(half * HEAD_SIZE, HEAD_SIZE)],
            (kvsend, kvrecv), (a, d, half), peer(base + up(d)))

    def q_copy(c, d, to):
        _, first, count = CHUNKS[c]
        return send(
            q.at[:, pl.ds(up(d) * Q_COLS + first * HEAD_SIZE, count * HEAD_SIZE)],
            qbuf.at[to, :, pl.ds(first * HEAD_SIZE, count * HEAD_SIZE)], (qsend, qrecv), (c, d), peer(base + up(d)))

    def c_copy(c, d, to):
        _, first, count = CHUNKS[c]
        return send(
            cot.at[:, :, pl.ds(up(d) * Q_COLS + first * HEAD_SIZE, count * HEAD_SIZE)],
            cbuf.at[to, :, :, pl.ds(first * HEAD_SIZE, count * HEAD_SIZE)], (csend, crecv), (c, d), peer(base + up(d)))

    def meta_copy(d, to):
        return send(meta, kvbuf0.at[to, pl.ds(TOK, META)], (msend, mrecv), d, peer(base + up(d)))

    def z_copy(a, i, first):
        ref = kvbuf[a].at[first + i]
        return send(ref, ref, (zsend, zrecv), (a, i), peer(zhere))

    def y_copy(a, d, first):
        ref = kvbuf[a].at[pl.ds(first, RING)]
        return send(ref, ref, (ysend, yrecv), (a, d), y_peer(d))

    def y_forward(a, d, first):
        ref = kvbuf[a].at[pl.ds(first + (0 if d == 1 else 2), 2)]
        return send(ref, ref, (yfsend, yfrecv), (a, d), y_peer(d))

    def yz_copy(a, d, i, first):
        ref = kvbuf[a].at[first + i]
        return send(ref, ref, (yzsend, yzrecv), (a, d, i), y_peer(d))

    def yz_forward(a, i, first):
        ref = kvbuf[a].at[first + i]
        return send(ref, ref, (yzfsend, yzfrecv), (a, i), y_peer(forward_way(i)))

    def place_cols(c, place):
        _, first, count = CHUNKS[c]
        return pl.ds(pl.multiple_of(lax.rem(place, RING) * Q_COLS + first * HEAD_SIZE, 128), count * HEAD_SIZE)

    def chunk_cols(c):
        _, first, count = CHUNKS[c]
        return pl.ds(first * HEAD_SIZE, count * HEAD_SIZE)

    def o_copy(c, d, target, source):
        return send(
            slots.at[target, :, chunk_cols(c)], owned.at[source // RING, :, place_cols(c, source)],
            (osend, orecv), (c, d), owner(target))

    def o_local(c):
        return pltpu.make_async_copy(
            slots.at[me, :, chunk_cols(c)], owned.at[here // RING, :, place_cols(c, here)], loc.at[c, 2])

    def kv_local(a, half):
        return pltpu.make_async_copy(
            kv.at[:, pl.ds((half * RING + x) * K_COLS + a * HEAD_SIZE, HEAD_SIZE)],
            kvbuf[a].at[here, pl.ds(0, TOK), pl.ds(half * HEAD_SIZE, HEAD_SIZE)], loc.at[a, 3 + half])

    def q_local(c):
        _, first, count = CHUNKS[c]
        return pltpu.make_async_copy(
            q.at[:, pl.ds(x * Q_COLS + first * HEAD_SIZE, count * HEAD_SIZE)], qbuf.at[x, :, chunk_cols(c)], loc.at[c, 0])

    def c_local(c):
        _, first, count = CHUNKS[c]
        return pltpu.make_async_copy(
            cot.at[:, :, pl.ds(x * Q_COLS + first * HEAD_SIZE, count * HEAD_SIZE)],
            cbuf.at[x, :, :, chunk_cols(c)], loc.at[c, 1])

    meta_local = pltpu.make_async_copy(meta, kvbuf0.at[here, pl.ds(TOK, META)], loc.at[0, 5])

    def tables(place):
        return kvbuf0[place, TOK: TOK + META, :].astype(F32)

    barrier = pltpu.get_barrier_semaphore()

    @pl.loop(1, OWNERS)
    def _(d):
        pl.semaphore_signal(barrier, inc=1, device_id=owner(lax.rem(me + d, OWNERS)), device_id_type=MESH)

    @pl.loop(1, LINE)
    def _(d):
        pl.semaphore_signal(barrier, inc=1, device_id=line_peer(d), device_id_type=MESH)

    pl.semaphore_signal(barrier, inc=1, device_id=core_peer, device_id_type=MESH)

    meta_local.start()
    for a in range(KV_LOCAL):
        for half in range(2):
            kv_local(a, half).start()
    for c in range(len(CHUNKS)):
        q_local(c).start()
        c_local(c).start()
    acc[...] = jnp.zeros_like(acc)
    for a in range(KV_LOCAL):
        kvs[a, pl.ds(0, BEHIND), :] = jnp.zeros((BEHIND, 2 * HEAD_SIZE), BF16)
    pl.semaphore_wait(barrier, OWNERS - 1 + LINE - 1 + 1)

    for d in directions:
        for half in range(2):
            kv_copy(0, d, half, here).start()
        meta_copy(d, here).start()
    for d in directions:
        for half in range(2):
            kv_copy(1, d, half, here).start()

    def rows_of(place):
        return one_hot(tables(place)[2:3], TOK)

    def ring_rows(a, first):
        for i in range(2):
            halves = [
                turned_dot(rows_of(first + 2 * i + j), kvbuf[a][first + 2 * i + j, :TOK, :])
                .reshape(OWNERS, 8, 2 * HEAD_SIZE) for j in range(2)
            ]
            kvslots[a, :, pl.ds(pl.multiple_of(8 * first + 16 * i, 16), 16), :] = (
                jnp.concatenate(halves, axis=1).astype(BF16))

    def ring_into(c, buf, put):
        count = CHUNKS[c][2] * HEAD_SIZE

        for i in range(2):
            halves = [
                turned_dot(rows_of(base + 2 * i + j), buf(2 * i + j)).reshape(OWNERS, 8, count) for j in range(2)
            ]
            put[:, pl.ds(pl.multiple_of(16 * i, 16), 16), chunk_cols(c)] = jnp.concatenate(halves, axis=1).astype(BF16)

    def queries_in(c):
        ring_into(c, lambda s: qbuf[s, :, chunk_cols(c)], qslots)

    def cotangents_in(c):
        for p in range(2):
            ring_into(c, lambda s, p=p: cbuf[s, p, :, chunk_cols(c)], cslots.at[p])

    def wait_kv(a):
        for half in range(2):
            kv_local(a, half).wait()
        for d in directions:
            for half in range(2):
                kv_copy(a, d, half, base + down(d)).wait_recv()
            if a == 0:
                meta_copy(d, base + down(d)).wait_recv()
        if a == 0:
            meta_local.wait()

    def pass_z(a, pieces):
        for i in pieces:
            z_copy(a, i, zbase).wait_recv()
            for d in ways:
                yz_copy(a, d, i, zbase).start()

    def pass_y(a):
        for d in ways:
            y_copy(a, d, y_base(base, d)).wait_recv()
            y_forward(a, d, y_base(base, d)).start()

    def pass_yz(a):
        for i in range(RING):
            d = forward_way(i)
            yz_copy(a, d, i, y_base(zbase, d)).wait_recv()
            yz_forward(a, i, y_base(zbase, d)).start()

    slot_code = (lax.broadcasted_iota(jnp.int32, (SLOTS, TOK), 0) + base * 8).astype(F32)
    own_row = (lax.broadcasted_iota(jnp.int32, (SLOTS, TOK), 1) + BEHIND).astype(F32)
    key_at = lax.broadcasted_iota(jnp.int32, (SLOTS, WINDOW), 1).astype(F32)

    def mask(t):
        block = tables(turn(t))
        mine = slot_code == block[0:1, :TOK]
        row_at = jnp.sum(jnp.where(mine, own_row, 0.0), axis=1, keepdims=True)
        row_seg = jnp.sum(jnp.where(mine, block[1:2, :TOK], 0.0), axis=1, keepdims=True)
        key_seg = jnp.concatenate([block[:8], jnp.zeros((8, WINDOW - 256), F32)], axis=1)
        key_seg = pltpu.roll(key_seg, BEHIND, 1)
        for j in range(3):
            before = jnp.where(t + j >= 3, tables(turn(jnp.maximum(t + j - 3, 0)))[:8], 0.0)
            before = jnp.concatenate([before, jnp.zeros((8, WINDOW - 256), F32)], axis=1)
            key_seg += before if j == 0 else pltpu.roll(before, j * TOK, 1)
        allowed = (key_at <= row_at) & (key_seg[1:2] == row_seg)
        bias[t] = jnp.where(allowed, 0.0, -1e30)

    def last_keys(a):
        for i in range(RING):
            d = 4 - forward_way(i)
            yz_copy(a, d, i, y_base(zbase, d)).wait_recv()
        for d in ways:
            ring_rows(a, y_base(zbase, d))
        for d in ways:
            y_forward(a, d, y_base(base, 2)).wait_recv()
        ring_rows(a, y_base(base, 2))
        for i in range(RING):
            yz_forward(a, i, y_base(zbase, 2)).wait_recv()
        ring_rows(a, y_base(zbase, 2))

        @pl.loop(0, OWNERS // 4)
        def _(i):
            for j in range(4):
                t = 4 * i + j
                hot = one_hot(tables(turn(t))[0:1, :TOK], 256)
                kvs[a, pl.ds(pl.multiple_of(BEHIND + t * TOK, 64), TOK), :] = (
                    turned_dot(hot, kvslots[a, t]).astype(BF16))
                if a == 0:
                    mask(t)

    def wait_queries(c):
        q_local(c).wait()
        for d in directions:
            q_copy(c, d, down(d)).wait_recv()

    def wait_cotangents(c):
        c_local(c).wait()
        for d in directions:
            c_copy(c, d, down(d)).wait_recv()

    wait_kv(0)
    for i in range(RING):
        z_copy(0, i, base).start()
    for d in ways:
        y_copy(0, d, base).start()
    wait_kv(1)
    for i in range(RING):
        z_copy(1, i, base).start()

    for c in range(len(CHUNKS)):
        for d in directions:
            q_copy(c, d, x).start()
        for d in directions:
            c_copy(c, d, x).start()
    ring_rows(0, base)
    pass_z(0, (0, 1))
    pass_y(0)
    pass_z(0, (2, 3))
    for d in ways:
        y_copy(1, d, base).start()
    ring_rows(0, zbase)
    for d in ways:
        ring_rows(0, y_base(base, d))

    wait_queries(0)

    pass_yz(0)
    ring_rows(1, base)
    queries_in(0)
    pass_y(1)
    pass_z(1, range(RING))
    last_keys(0)

    wait_cotangents(0)
    cotangents_in(0)

    def attend(c, d, u):
        a, first, count = CHUNKS[c]
        t = lax.rem(me + d, OWNERS)
        start = pl.multiple_of(t * TOK, 64)

        def heads(ref):
            return jnp.concatenate(
                [ref[t, :, h * HEAD_SIZE: (h + 1) * HEAD_SIZE] for h in range(first, first + count)], axis=0)

        keys = kvs[a, pl.ds(start, WINDOW), :HEAD_SIZE]
        values = kvs[a, pl.ds(start, WINDOW), HEAD_SIZE:]
        scores = dot_t(heads(qslots), keys).reshape(count, SLOTS, WINDOW) + bias[t][None]
        top = jnp.max(scores, axis=2, keepdims=True)
        weights = jnp.exp2((scores - top) * exponent)
        probs = weights * (1.0 / jnp.sum(weights, axis=2, keepdims=True))
        mixed = jnp.dot(probs.astype(BF16).reshape(count * SLOTS, WINDOW), values, preferred_element_type=F32)
        for h in range(count):
            slots[t, :, (first + h) * HEAD_SIZE: (first + h + 1) * HEAD_SIZE] = (
                mixed[h * SLOTS: (h + 1) * SLOTS].astype(BF16))
        sums = []
        for p in range(2):
            upstream = heads(cslots.at[p])
            delta = jnp.sum(upstream.astype(F32) * mixed, axis=1, keepdims=True)
            grad = probs * (dot_t(upstream, values) - delta).reshape(count, SLOTS, WINDOW)
            sums.append(jnp.sum(grad.reshape(count, SLOTS // 8, 8, WINDOW), axis=1).reshape(count * 8, WINDOW))
        sums = jnp.concatenate(sums, axis=0)
        high = sums.astype(BF16)
        low = (sums - high.astype(F32)).astype(BF16)
        acc[c, u, : 4 * count * 8] += jnp.dot(jnp.concatenate([high, low], axis=0), keys, preferred_element_type=F32)

    def attend_some(c, begin, end):
        @pl.loop(begin, end)
        def _(i):
            for u in range(2):
                attend(c, 2 * i + u, u)

            @pl.when(i == 0)
            def _():
                o_local(c).start()

            @pl.when(i > 0)
            def _():
                o_copy(c, 2 * i, lax.rem(me + 2 * i, OWNERS), here).start()

            o_copy(c, 2 * i + 1, lax.rem(me + 2 * i + 1, OWNERS), here).start()

    attend_some(0, 0, OWNERS // 4)
    pass_yz(1)
    attend_some(0, OWNERS // 4, OWNERS // 2)

    ring_rows(1, zbase)
    for d in ways:
        ring_rows(1, y_base(base, d))
    last_keys(1)
    for c in (1,):
        wait_queries(c)
        queries_in(c)
        wait_cotangents(c)
        cotangents_in(c)
        attend_some(c, 0, OWNERS // 2)

    grads[...] = jnp.zeros_like(grads)
    for c, (_, first, count) in enumerate(CHUNKS):
        both = acc[c, 0] + acc[c, 1]
        step = count * 8
        for p in range(2):
            total = both[p * step: (p + 1) * step] + both[(2 + p) * step: (3 + p) * step]
            for h in range(count):
                row = jnp.sum(total[h * 8: (h + 1) * 8], axis=0, keepdims=True) * scale
                grads[pl.ds(p * 16 + first + h, 1), :] = row
    parts[pl.ds(line, 1)] = grads[...][None]

    def g_copy(d, at):
        return send(parts.at[at], parts.at[at], (gsend, grecv), d, line_peer(d))

    def b_copy(d, at):
        return send(yparts.at[at], yparts.at[at], (bsend, brecv), d, y_peer(d))

    def x_copy(d, at):
        return send(xparts.at[at], xparts.at[at], (xsend, xrecv), d, peer(base + up(d)))

    def p_copy(at):
        return send(cparts.at[at], cparts.at[at], (psend, precv), 0, core_peer)

    def into_rows(c):
        hot = one_hot(tables(here)[0:1, :TOK], 256)
        o_local(c).wait()

        @pl.loop(1, OWNERS)
        def _(d):
            o_copy(c, d, me, turn(lax.rem(me + OWNERS - d, OWNERS))).wait_recv()

        _, first, count = CHUNKS[c]
        for g in range(RING):
            cols = pl.ds(g * Q_COLS + first * HEAD_SIZE, count * HEAD_SIZE)
            result[:, cols] = turned_dot(hot, owned[:, :, cols].reshape(256, count * HEAD_SIZE)).astype(BF16)

    @pl.loop(1, LINE)
    def _(d):
        g_copy(d, line).start()


    @pl.loop(1, LINE)
    def _(d):
        g_copy(d, lax.rem(line + LINE - d, LINE)).wait_recv()
        g_copy(d, line).wait_send()

    yparts[pl.ds(y, 1)] = jnp.sum(parts[...], axis=0)[None]
    for d in directions:
        b_copy(d, y).start()
    for d in directions:
        b_copy(d, lax.rem(y + RING - d, RING)).wait_recv()
        b_copy(d, y).wait_send()
    xparts[pl.ds(x, 1)] = jnp.sum(yparts[...], axis=0)[None]
    for d in directions:
        x_copy(d, x).start()
    into_rows(0)
    for d in directions:
        x_copy(d, down(d)).wait_recv()
        x_copy(d, x).wait_send()
    cparts[pl.ds(core, 1)] = xparts[...][None]
    p_copy(core).start()
    p_copy(1 - core).wait_recv()
    p_copy(core).wait_send()
    total = cparts[0] + cparts[1]
    for g in range(RING):
        square = (total[g, :16] * total[g, :16] + total[g, 16:] * total[g, 16:]) / token_total
        heads_here = QUERY_HEADS // RING
        curve[g * heads_here: (g + 1) * heads_here, :] = square[:heads_here]
    into_rows(1)

    for d in directions:
        meta_copy(d, here).wait_send()

    @pl.loop(1, OWNERS)
    def _(d):
        for c in range(len(CHUNKS)):
            o_copy(c, d, lax.rem(me + d, OWNERS), here).wait_send()

    for c in range(len(CHUNKS)):
        for d in directions:
            q_copy(c, d, x).wait_send()
            c_copy(c, d, x).wait_send()
    for a in range(KV_LOCAL):
        for d in directions:
            for half in range(2):
                kv_copy(a, d, half, here).wait_send()
        for d in ways:
            y_copy(a, d, base).wait_send()
            y_forward(a, d, y_base(base, d)).wait_send()
            for i in range(RING):
                yz_copy(a, d, i, zbase).wait_send()
        for i in range(RING):
            z_copy(a, i, base).wait_send()
            yz_forward(a, i, y_base(zbase, forward_way(i))).wait_send()


def run(q, kv, cot, meta, token_total):
    hbm = pl.BlockSpec(memory_space=pl.ANY)
    vmem = pl.BlockSpec(memory_space=pltpu.VMEM)
    n = len(CHUNKS)

    def dma(*shape):
        return [pltpu.SemaphoreType.DMA(shape)] * 2

    return pl.pallas_call(
        functools.partial(kernel, token_total),
        out_shape=(
            jax.ShapeDtypeStruct((TOK, RING * Q_COLS), BF16),
            jax.ShapeDtypeStruct((QUERY_HEADS, HEAD_SIZE), F32),
        ),
        in_specs=[hbm] * 4,
        out_specs=(vmem, vmem),
        scratch_shapes=[
            pltpu.VMEM((RING, TOK, Q_COLS), BF16),
            pltpu.VMEM((RING, 2, TOK, Q_COLS), BF16),
            pltpu.VMEM((OWNERS, TOK + META, 2 * HEAD_SIZE), BF16),
            pltpu.VMEM((OWNERS, TOK, 2 * HEAD_SIZE), BF16),
            pltpu.VMEM((OWNERS, SLOTS, Q_COLS), BF16),
            pltpu.VMEM((2, OWNERS, SLOTS, Q_COLS), BF16),
            pltpu.VMEM((KV_LOCAL, OWNERS, 256, 2 * HEAD_SIZE), BF16),
            pltpu.VMEM((KV_LOCAL, BEHIND + OWNERS * TOK, 2 * HEAD_SIZE), BF16),
            pltpu.VMEM((OWNERS, SLOTS, WINDOW), F32),
            pltpu.VMEM((OWNERS, SLOTS, Q_COLS), BF16),
            pltpu.VMEM((OWNERS // RING, SLOTS, RING * Q_COLS), BF16),
            pltpu.VMEM((n, 2, 4 * GROUP * 8, HEAD_SIZE), F32),
            pltpu.VMEM((32, HEAD_SIZE), F32),
            pltpu.VMEM((LINE, 32, HEAD_SIZE), F32),
            pltpu.VMEM((RING, 32, HEAD_SIZE), F32),
            pltpu.VMEM((RING, 32, HEAD_SIZE), F32),
            pltpu.VMEM((2, RING, 32, HEAD_SIZE), F32),
            pltpu.SemaphoreType.DMA((n, 6)),
            *dma(KV_LOCAL, RING, 2), *dma(RING), *dma(n, RING), *dma(n, RING),
            *dma(KV_LOCAL, RING), *dma(KV_LOCAL, RING), *dma(KV_LOCAL, RING),
            *dma(KV_LOCAL, RING, RING), *dma(KV_LOCAL, RING), *dma(n, OWNERS),
            *dma(LINE), *dma(RING), *dma(RING), *dma(1),
        ],
        compiler_params=pltpu.CompilerParams(collective_id=0, has_side_effects=True, vmem_limit_bytes=VMEM),
        name="curvature",
    )(q, kv, cot, meta)


def per_device(queries, packed_keys_values, cotangents, send_rows, take_slots, segment_ids):
    sender = take_slots // CAP
    turned = (sender % 4) * 8 + (sender // 4 % 2) * 4 + sender // 8
    code = jnp.where(lax.axis_index("dp") % 2 == 0, sender, turned) * 8 + take_slots % CAP
    meta = jnp.concatenate([
        jnp.pad(code, ((0, 0), (0, 256 - TOK))),
        jnp.pad(segment_ids + 1, ((0, 0), (0, 256 - TOK))),
        jnp.pad(send_rows[0, 0], ((0, 0), (0, 8 - CAP)), constant_values=-1).reshape(1, 256),
        jnp.zeros((META - 3, 256), jnp.int32),
    ], axis=0).astype(BF16)
    cot = jnp.transpose(cotangents[0], (1, 0, 2))
    token_total = 2.0 * TOK * OWNERS * lax.axis_size("dp")
    out, curve = run(queries[0], packed_keys_values[0], cot, meta, token_total)
    return out[None], curve.reshape(-1)


def solution(mesh):
    placed = (
        P("dp", "ctx", None),
        P("dp", "ctx", None),
        P("dp", "ctx", None, None),
        P("dp", "ctx", None, None),
        P("dp", "ctx"),
        P("dp", "ctx"),
    )
    return jax.shard_map(
        per_device,
        mesh=mesh,
        in_specs=placed,
        out_specs=(P("dp", "ctx", None), P()),
        check_vma=False,
    )
```

```python
import functools
import math

import jax
import jax.numpy as jnp
from jax import lax
from jax.experimental import pallas as pl
from jax.experimental.pallas import tpu as pltpu
from jax.sharding import PartitionSpec as P

QUERY_HEADS = 40
KEY_VALUE_HEADS = 8
HEAD_SIZE = 128
TOK = 192
META = 16
CAP = 7
OWNERS = 32
RING = 4
GROUP = QUERY_HEADS // KEY_VALUE_HEADS
KV_LOCAL = KEY_VALUE_HEADS // RING
Q_COLS = QUERY_HEADS * HEAD_SIZE // RING
K_COLS = KV_LOCAL * HEAD_SIZE
SLOTS = 8 * RING
WINDOW = 4 * TOK
BEHIND = 3 * TOK
LINE = 8
CHUNKS = ((0, 0, 5), (1, 5, 5))
VMEM = 60 * 1024 * 1024
MESH = pl.DeviceIdType.MESH
F32 = jnp.float32
BF16 = jnp.bfloat16


def turned_dot(a, b):
    return lax.dot_general(a, b, (((0,), (0,)), ((), ())), preferred_element_type=F32)


def dot_t(a, b):
    return lax.dot_general(a, b, (((1,), (1,)), ((), ())), preferred_element_type=F32)


def one_hot(row, count):
    iota = lax.broadcasted_iota(jnp.int32, (count, row.shape[1]), 0).astype(F32)
    return jnp.where(iota == row, 1.0, 0.0).astype(BF16)


def kernel(token_total, q, kv, cot, meta, result, curve,
           cotraw, cotp, qbuf, cbuf, kvbuf0, kvbuf1, qslots, cslots, kvslots, kvs, bias, slots, owned, acc, grads,
           parts, yparts, xparts, cparts,
           loc, kvsend, kvrecv, msend, mrecv, qsend, qrecv, csend, crecv, zsend, zrecv, ysend, yrecv, yfsend, yfrecv,
           yzsend, yzrecv, yzfsend, yzfrecv, osend, orecv, gsend, grecv, bsend, brecv, xsend, xrecv, psend, precv):
    kvbuf = (kvbuf0, kvbuf1)
    me = lax.axis_index("ctx")
    dp = lax.axis_index("dp")
    core = lax.rem(dp, 2)
    scale = 1.0 / math.sqrt(HEAD_SIZE)
    exponent = scale * math.log2(math.e)

    def turn(n):
        fast, slow = lax.rem(n, 4), n // 8
        return (slow + core * (fast - slow)) * 8 + lax.rem(n // 4, 2) * 4 + fast + core * (slow - fast)

    here = turn(me)
    x = lax.rem(here, RING)
    base = here - x
    zoff = lax.rem(here // 4, 2)
    y = here // 8
    zhere = here + 4 - 8 * zoff
    zbase = zhere - x
    line = zoff * 4 + dp // 2
    directions = (1, 3, 2)
    ways = (1, 3)

    def peer(place):
        return (dp, turn(place))

    def owner(t):
        return (dp, t)

    def line_peer(d):
        n = lax.rem(line + d, LINE)
        return (lax.rem(n, 4) * 2 + core, me + 4 * (n // 4 - zoff))

    core_peer = (dp + 1 - 2 * core, me)

    def up(d):
        return lax.rem(x + d, RING)

    def down(d):
        return lax.rem(x + RING - d, RING)

    def y_peer(d):
        return peer(lax.rem(here + 8 * d, OWNERS))

    def y_base(first, d):
        return lax.rem(first + OWNERS - 8 * d, OWNERS)

    def forward_way(i):
        return 1 if i < 2 else 3

    def send(src, dst, sems, at, device):
        return pltpu.make_async_remote_copy(
            src, dst, sems[0].at[at], sems[1].at[at], device_id=device, device_id_type=MESH)

    def kv_copy(a, d, half, to):
        return send(
            kv.at[:, pl.ds((half * RING + up(d)) * K_COLS + a * HEAD_SIZE, HEAD_SIZE)],
            kvbuf[a].at[to, pl.ds(0, TOK), pl.ds(half * HEAD_SIZE, HEAD_SIZE)],
            (kvsend, kvrecv), (a, d, half), peer(base + up(d)))

    def q_copy(c, d, to):
        _, first, count = CHUNKS[c]
        return send(
            q.at[:, pl.ds(up(d) * Q_COLS + first * HEAD_SIZE, count * HEAD_SIZE)],
            qbuf.at[to, :, pl.ds(first * HEAD_SIZE, count * HEAD_SIZE)], (qsend, qrecv), (c, d), peer(base + up(d)))

    def c_copy(c, d, to):
        _, first, count = CHUNKS[c]
        return send(
            cotp.at[:, :, pl.ds(up(d) * Q_COLS + first * HEAD_SIZE, count * HEAD_SIZE)],
            cbuf.at[to, :, :, pl.ds(first * HEAD_SIZE, count * HEAD_SIZE)], (csend, crecv), (c, d), peer(base + up(d)))

    def meta_copy(d, to):
        return send(meta, kvbuf0.at[to, pl.ds(TOK, META)], (msend, mrecv), d, peer(base + up(d)))

    def z_copy(a, i, first):
        ref = kvbuf[a].at[first + i]
        return send(ref, ref, (zsend, zrecv), (a, i), peer(zhere))

    def y_copy(a, d, first):
        ref = kvbuf[a].at[pl.ds(first, RING)]
        return send(ref, ref, (ysend, yrecv), (a, d), y_peer(d))

    def y_forward(a, d, first):
        ref = kvbuf[a].at[pl.ds(first + (0 if d == 1 else 2), 2)]
        return send(ref, ref, (yfsend, yfrecv), (a, d), y_peer(d))

    def yz_copy(a, d, i, first):
        ref = kvbuf[a].at[first + i]
        return send(ref, ref, (yzsend, yzrecv), (a, d, i), y_peer(d))

    def yz_forward(a, i, first):
        ref = kvbuf[a].at[first + i]
        return send(ref, ref, (yzfsend, yzfrecv), (a, i), y_peer(forward_way(i)))

    def place_cols(c, place):
        _, first, count = CHUNKS[c]
        return pl.ds(pl.multiple_of(lax.rem(place, RING) * Q_COLS + first * HEAD_SIZE, 128), count * HEAD_SIZE)

    def chunk_cols(c):
        _, first, count = CHUNKS[c]
        return pl.ds(first * HEAD_SIZE, count * HEAD_SIZE)

    def o_copy(c, d, target, source):
        return send(
            slots.at[target, :, chunk_cols(c)], owned.at[source // RING, :, place_cols(c, source)],
            (osend, orecv), (c, d), owner(target))

    def o_local(c):
        return pltpu.make_async_copy(
            slots.at[me, :, chunk_cols(c)], owned.at[here // RING, :, place_cols(c, here)], loc.at[c, 2])

    def kv_local(a, half):
        return pltpu.make_async_copy(
            kv.at[:, pl.ds((half * RING + x) * K_COLS + a * HEAD_SIZE, HEAD_SIZE)],
            kvbuf[a].at[here, pl.ds(0, TOK), pl.ds(half * HEAD_SIZE, HEAD_SIZE)], loc.at[a, 3 + half])

    def q_local(c):
        _, first, count = CHUNKS[c]
        return pltpu.make_async_copy(
            q.at[:, pl.ds(x * Q_COLS + first * HEAD_SIZE, count * HEAD_SIZE)], qbuf.at[x, :, chunk_cols(c)], loc.at[c, 0])

    def c_local(c):
        _, first, count = CHUNKS[c]
        return pltpu.make_async_copy(
            cotp.at[:, :, pl.ds(x * Q_COLS + first * HEAD_SIZE, count * HEAD_SIZE)],
            cbuf.at[x, :, :, chunk_cols(c)], loc.at[c, 1])

    meta_local = pltpu.make_async_copy(meta, kvbuf0.at[here, pl.ds(TOK, META)], loc.at[0, 5])

    cot_local = pltpu.make_async_copy(cot, cotraw, loc.at[1, 5])

    def tables(place):
        return kvbuf0[place, TOK: TOK + META, :].astype(F32)

    barrier = pltpu.get_barrier_semaphore()

    @pl.loop(1, OWNERS)
    def _(d):
        pl.semaphore_signal(barrier, inc=1, device_id=owner(lax.rem(me + d, OWNERS)), device_id_type=MESH)

    @pl.loop(1, LINE)
    def _(d):
        pl.semaphore_signal(barrier, inc=1, device_id=line_peer(d), device_id_type=MESH)

    pl.semaphore_signal(barrier, inc=1, device_id=core_peer, device_id_type=MESH)

    meta_local.start()
    for a in range(KV_LOCAL):
        for half in range(2):
            kv_local(a, half).start()
    for c in range(len(CHUNKS)):
        q_local(c).start()
    cot_local.start()
    acc[...] = jnp.zeros_like(acc)
    for a in range(KV_LOCAL):
        kvs[a, pl.ds(0, BEHIND), :] = jnp.zeros((BEHIND, 2 * HEAD_SIZE), BF16)
    pl.semaphore_wait(barrier, OWNERS - 1 + LINE - 1 + 1)

    for d in directions:
        for half in range(2):
            kv_copy(0, d, half, here).start()
        meta_copy(d, here).start()
    for d in directions:
        for half in range(2):
            kv_copy(1, d, half, here).start()

    def rows_of(place):
        return one_hot(tables(place)[2:3], TOK)

    def ring_rows(a, first):
        for i in range(2):
            halves = [
                turned_dot(rows_of(first + 2 * i + j), kvbuf[a][first + 2 * i + j, :TOK, :])
                .reshape(OWNERS, 8, 2 * HEAD_SIZE) for j in range(2)
            ]
            kvslots[a, :, pl.ds(pl.multiple_of(8 * first + 16 * i, 16), 16), :] = (
                jnp.concatenate(halves, axis=1).astype(BF16))

    def ring_into(c, buf, put):
        count = CHUNKS[c][2] * HEAD_SIZE

        for i in range(2):
            halves = [
                turned_dot(rows_of(base + 2 * i + j), buf(2 * i + j)).reshape(OWNERS, 8, count) for j in range(2)
            ]
            put[:, pl.ds(pl.multiple_of(16 * i, 16), 16), chunk_cols(c)] = jnp.concatenate(halves, axis=1).astype(BF16)

    def queries_in(c):
        ring_into(c, lambda s: qbuf[s, :, chunk_cols(c)], qslots)

    def cotangents_in(c):
        for p in range(2):
            ring_into(c, lambda s, p=p: cbuf[s, p, :, chunk_cols(c)], cslots.at[p])

    def wait_kv(a):
        for half in range(2):
            kv_local(a, half).wait()
        for d in directions:
            for half in range(2):
                kv_copy(a, d, half, base + down(d)).wait_recv()
            if a == 0:
                meta_copy(d, base + down(d)).wait_recv()
        if a == 0:
            meta_local.wait()

    def pass_z(a, pieces):
        for i in pieces:
            z_copy(a, i, zbase).wait_recv()
            for d in ways:
                yz_copy(a, d, i, zbase).start()

    def pass_y(a):
        for d in ways:
            y_copy(a, d, y_base(base, d)).wait_recv()
            y_forward(a, d, y_base(base, d)).start()

    def pass_yz(a):
        for i in range(RING):
            d = forward_way(i)
            yz_copy(a, d, i, y_base(zbase, d)).wait_recv()
            yz_forward(a, i, y_base(zbase, d)).start()

    slot_code = (lax.broadcasted_iota(jnp.int32, (SLOTS, TOK), 0) + base * 8).astype(F32)
    own_row = (lax.broadcasted_iota(jnp.int32, (SLOTS, TOK), 1) + BEHIND).astype(F32)
    key_at = lax.broadcasted_iota(jnp.int32, (SLOTS, WINDOW), 1).astype(F32)

    def mask(t):
        block = tables(turn(t))
        mine = slot_code == block[0:1, :TOK]
        row_at = jnp.sum(jnp.where(mine, own_row, 0.0), axis=1, keepdims=True)
        row_seg = jnp.sum(jnp.where(mine, block[1:2, :TOK], 0.0), axis=1, keepdims=True)
        key_seg = jnp.concatenate([block[:8], jnp.zeros((8, WINDOW - 256), F32)], axis=1)
        key_seg = pltpu.roll(key_seg, BEHIND, 1)
        for j in range(3):
            before = jnp.where(t + j >= 3, tables(turn(jnp.maximum(t + j - 3, 0)))[:8], 0.0)
            before = jnp.concatenate([before, jnp.zeros((8, WINDOW - 256), F32)], axis=1)
            key_seg += before if j == 0 else pltpu.roll(before, j * TOK, 1)
        allowed = (key_at <= row_at) & (key_seg[1:2] == row_seg)
        bias[t] = jnp.where(allowed, 0.0, -1e30)

    def last_keys(a):
        for i in range(RING):
            d = 4 - forward_way(i)
            yz_copy(a, d, i, y_base(zbase, d)).wait_recv()
        for d in ways:
            ring_rows(a, y_base(zbase, d))
        for d in ways:
            y_forward(a, d, y_base(base, 2)).wait_recv()
        ring_rows(a, y_base(base, 2))
        for i in range(RING):
            yz_forward(a, i, y_base(zbase, 2)).wait_recv()
        ring_rows(a, y_base(zbase, 2))

        @pl.loop(0, OWNERS // 4)
        def _(i):
            for j in range(4):
                t = 4 * i + j
                hot = one_hot(tables(turn(t))[0:1, :TOK], 256)
                kvs[a, pl.ds(pl.multiple_of(BEHIND + t * TOK, 64), TOK), :] = (
                    turned_dot(hot, kvslots[a, t]).astype(BF16))
                if a == 0:
                    mask(t)

    def wait_queries(c):
        q_local(c).wait()
        for d in directions:
            q_copy(c, d, down(d)).wait_recv()

    def wait_cotangents(c):
        c_local(c).wait()
        for d in directions:
            c_copy(c, d, down(d)).wait_recv()

    wait_kv(0)
    for i in range(RING):
        z_copy(0, i, base).start()
    for d in ways:
        y_copy(0, d, base).start()
    wait_kv(1)
    for i in range(RING):
        z_copy(1, i, base).start()

    for d in directions:
        q_copy(0, d, x).start()
    cot_local.wait()

    @pl.loop(0, TOK // 16)
    def _(i):
        rows = pl.ds(pl.multiple_of(16 * i, 16), 16)
        for p in range(2):
            cotp[p, rows, :] = cotraw[rows, p, :]

    for c in range(len(CHUNKS)):
        c_local(c).start()
    for d in directions:
        c_copy(0, d, x).start()
    ring_rows(0, base)
    pass_z(0, (0, 1))
    pass_y(0)
    pass_z(0, (2, 3))
    for d in ways:
        y_copy(1, d, base).start()
    ring_rows(0, zbase)
    for d in ways:
        ring_rows(0, y_base(base, d))

    wait_queries(0)
    for d in directions:
        q_copy(1, d, x).start()

    pass_yz(0)
    ring_rows(1, base)
    queries_in(0)
    pass_y(1)
    pass_z(1, range(RING))
    last_keys(0)
    ring_rows(1, zbase)
    for d in ways:
        ring_rows(1, y_base(base, d))

    wait_cotangents(0)
    for d in directions:
        c_copy(1, d, x).start()
    cotangents_in(0)

    def attend(c, d, u):
        a, first, count = CHUNKS[c]
        t = lax.rem(me + d, OWNERS)
        start = pl.multiple_of(t * TOK, 64)

        def heads(ref):
            return jnp.concatenate(
                [ref[t, :, h * HEAD_SIZE: (h + 1) * HEAD_SIZE] for h in range(first, first + count)], axis=0)

        keys = kvs[a, pl.ds(start, WINDOW), :HEAD_SIZE]
        values = kvs[a, pl.ds(start, WINDOW), HEAD_SIZE:]
        scores = dot_t(heads(qslots), keys).reshape(count, SLOTS, WINDOW) + bias[t][None]
        top = jnp.max(scores, axis=2, keepdims=True)
        weights = jnp.exp2((scores - top) * exponent)
        probs = weights * (1.0 / jnp.sum(weights, axis=2, keepdims=True))
        mixed = jnp.dot(probs.astype(BF16).reshape(count * SLOTS, WINDOW), values, preferred_element_type=F32)
        for h in range(count):
            slots[t, :, (first + h) * HEAD_SIZE: (first + h + 1) * HEAD_SIZE] = (
                mixed[h * SLOTS: (h + 1) * SLOTS].astype(BF16))
        sums = []
        for p in range(2):
            upstream = heads(cslots.at[p])
            delta = jnp.sum(upstream.astype(F32) * mixed, axis=1, keepdims=True)
            grad = probs * (dot_t(upstream, values) - delta).reshape(count, SLOTS, WINDOW)
            sums.append(jnp.sum(grad.reshape(count, SLOTS // 8, 8, WINDOW), axis=1).reshape(count * 8, WINDOW))
        sums = jnp.concatenate(sums, axis=0)
        high = sums.astype(BF16)
        low = (sums - high.astype(F32)).astype(BF16)
        acc[c, u, : 4 * count * 8] += jnp.dot(jnp.concatenate([high, low], axis=0), keys, preferred_element_type=F32)

    def attend_some(c, begin, end):
        @pl.loop(begin, end)
        def _(i):
            for u in range(2):
                attend(c, 2 * i + u, u)

            @pl.when(i == 0)
            def _():
                o_local(c).start()

            @pl.when(i > 0)
            def _():
                o_copy(c, 2 * i, lax.rem(me + 2 * i, OWNERS), here).start()

            o_copy(c, 2 * i + 1, lax.rem(me + 2 * i + 1, OWNERS), here).start()

    attend_some(0, 0, OWNERS // 4)
    pass_yz(1)
    attend_some(0, OWNERS // 4, OWNERS // 2)

    last_keys(1)
    for c in (1,):
        wait_queries(c)
        queries_in(c)
        wait_cotangents(c)
        cotangents_in(c)
        attend_some(c, 0, OWNERS // 2)

    grads[...] = jnp.zeros_like(grads)
    for c, (_, first, count) in enumerate(CHUNKS):
        both = acc[c, 0] + acc[c, 1]
        step = count * 8
        for p in range(2):
            total = both[p * step: (p + 1) * step] + both[(2 + p) * step: (3 + p) * step]
            for h in range(count):
                row = jnp.sum(total[h * 8: (h + 1) * 8], axis=0, keepdims=True) * scale
                grads[pl.ds(p * 16 + first + h, 1), :] = row
    parts[pl.ds(line, 1)] = grads[...][None]

    def g_copy(d, at):
        return send(parts.at[at], parts.at[at], (gsend, grecv), d, line_peer(d))

    def b_copy(d, at):
        return send(yparts.at[at], yparts.at[at], (bsend, brecv), d, y_peer(d))

    def x_copy(d, at):
        return send(xparts.at[at], xparts.at[at], (xsend, xrecv), d, peer(base + up(d)))

    def p_copy(at):
        return send(cparts.at[at], cparts.at[at], (psend, precv), 0, core_peer)

    def into_rows(c):
        hot = one_hot(tables(here)[0:1, :TOK], 256)
        o_local(c).wait()

        @pl.loop(1, OWNERS)
        def _(d):
            o_copy(c, d, me, turn(lax.rem(me + OWNERS - d, OWNERS))).wait_recv()

        _, first, count = CHUNKS[c]
        for g in range(RING):
            cols = pl.ds(g * Q_COLS + first * HEAD_SIZE, count * HEAD_SIZE)
            result[:, cols] = turned_dot(hot, owned[:, :, cols].reshape(256, count * HEAD_SIZE)).astype(BF16)

    @pl.loop(1, LINE)
    def _(d):
        g_copy(d, line).start()


    @pl.loop(1, LINE)
    def _(d):
        g_copy(d, lax.rem(line + LINE - d, LINE)).wait_recv()
        g_copy(d, line).wait_send()

    yparts[pl.ds(y, 1)] = jnp.sum(parts[...], axis=0)[None]
    for d in directions:
        b_copy(d, y).start()
    for d in directions:
        b_copy(d, lax.rem(y + RING - d, RING)).wait_recv()
        b_copy(d, y).wait_send()
    xparts[pl.ds(x, 1)] = jnp.sum(yparts[...], axis=0)[None]
    for d in directions:
        x_copy(d, x).start()
    into_rows(0)
    for d in directions:
        x_copy(d, down(d)).wait_recv()
        x_copy(d, x).wait_send()
    cparts[pl.ds(core, 1)] = xparts[...][None]
    p_copy(core).start()
    p_copy(1 - core).wait_recv()
    p_copy(core).wait_send()
    total = cparts[0] + cparts[1]
    for g in range(RING):
        square = (total[g, :16] * total[g, :16] + total[g, 16:] * total[g, 16:]) / token_total
        heads_here = QUERY_HEADS // RING
        curve[g * heads_here: (g + 1) * heads_here, :] = square[:heads_here]
    into_rows(1)

    for d in directions:
        meta_copy(d, here).wait_send()

    @pl.loop(1, OWNERS)
    def _(d):
        for c in range(len(CHUNKS)):
            o_copy(c, d, lax.rem(me + d, OWNERS), here).wait_send()

    for c in range(len(CHUNKS)):
        for d in directions:
            q_copy(c, d, x).wait_send()
            c_copy(c, d, x).wait_send()
    for a in range(KV_LOCAL):
        for d in directions:
            for half in range(2):
                kv_copy(a, d, half, here).wait_send()
        for d in ways:
            y_copy(a, d, base).wait_send()
            y_forward(a, d, y_base(base, d)).wait_send()
            for i in range(RING):
                yz_copy(a, d, i, zbase).wait_send()
        for i in range(RING):
            z_copy(a, i, base).wait_send()
            yz_forward(a, i, y_base(zbase, forward_way(i))).wait_send()


def run(q, kv, cot, meta, token_total):
    hbm = pl.BlockSpec(memory_space=pl.ANY)
    vmem = pl.BlockSpec(memory_space=pltpu.VMEM)
    n = len(CHUNKS)

    def dma(*shape):
        return [pltpu.SemaphoreType.DMA(shape)] * 2

    return pl.pallas_call(
        functools.partial(kernel, token_total),
        out_shape=(
            jax.ShapeDtypeStruct((TOK, RING * Q_COLS), BF16),
            jax.ShapeDtypeStruct((QUERY_HEADS, HEAD_SIZE), F32),
        ),
        in_specs=[hbm] * 4,
        out_specs=(vmem, vmem),
        scratch_shapes=[
            pltpu.VMEM((TOK, 2, RING * Q_COLS), BF16),
            pltpu.VMEM((2, TOK, RING * Q_COLS), BF16),
            pltpu.VMEM((RING, TOK, Q_COLS), BF16),
            pltpu.VMEM((RING, 2, TOK, Q_COLS), BF16),
            pltpu.VMEM((OWNERS, TOK + META, 2 * HEAD_SIZE), BF16),
            pltpu.VMEM((OWNERS, TOK, 2 * HEAD_SIZE), BF16),
            pltpu.VMEM((OWNERS, SLOTS, Q_COLS), BF16),
            pltpu.VMEM((2, OWNERS, SLOTS, Q_COLS), BF16),
            pltpu.VMEM((KV_LOCAL, OWNERS, 256, 2 * HEAD_SIZE), BF16),
            pltpu.VMEM((KV_LOCAL, BEHIND + OWNERS * TOK, 2 * HEAD_SIZE), BF16),
            pltpu.VMEM((OWNERS, SLOTS, WINDOW), F32),
            pltpu.VMEM((OWNERS, SLOTS, Q_COLS), BF16),
            pltpu.VMEM((OWNERS // RING, SLOTS, RING * Q_COLS), BF16),
            pltpu.VMEM((n, 2, 4 * GROUP * 8, HEAD_SIZE), F32),
            pltpu.VMEM((32, HEAD_SIZE), F32),
            pltpu.VMEM((LINE, 32, HEAD_SIZE), F32),
            pltpu.VMEM((RING, 32, HEAD_SIZE), F32),
            pltpu.VMEM((RING, 32, HEAD_SIZE), F32),
            pltpu.VMEM((2, RING, 32, HEAD_SIZE), F32),
            pltpu.SemaphoreType.DMA((n, 6)),
            *dma(KV_LOCAL, RING, 2), *dma(RING), *dma(n, RING), *dma(n, RING),
            *dma(KV_LOCAL, RING), *dma(KV_LOCAL, RING), *dma(KV_LOCAL, RING),
            *dma(KV_LOCAL, RING, RING), *dma(KV_LOCAL, RING), *dma(n, OWNERS),
            *dma(LINE), *dma(RING), *dma(RING), *dma(1),
        ],
        compiler_params=pltpu.CompilerParams(collective_id=0, has_side_effects=True, vmem_limit_bytes=VMEM),
        name="curvature",
    )(q, kv, cot, meta)


def per_device(queries, packed_keys_values, cotangents, send_rows, take_slots, segment_ids):
    sender = take_slots // CAP
    turned = (sender % 4) * 8 + (sender // 4 % 2) * 4 + sender // 8
    code = jnp.where(lax.axis_index("dp") % 2 == 0, sender, turned) * 8 + take_slots % CAP
    meta = jnp.concatenate([
        jnp.pad(code, ((0, 0), (0, 256 - TOK))),
        jnp.pad(segment_ids + 1, ((0, 0), (0, 256 - TOK))),
        jnp.pad(send_rows[0, 0], ((0, 0), (0, 8 - CAP)), constant_values=-1).reshape(1, 256),
        jnp.zeros((META - 3, 256), jnp.int32),
    ], axis=0).astype(BF16)
    token_total = 2.0 * TOK * OWNERS * lax.axis_size("dp")
    out, curve = run(queries[0], packed_keys_values[0], cotangents[0], meta, token_total)
    return out[None], curve.reshape(-1)


def solution(mesh):
    placed = (
        P("dp", "ctx", None),
        P("dp", "ctx", None),
        P("dp", "ctx", None, None),
        P("dp", "ctx", None, None),
        P("dp", "ctx"),
        P("dp", "ctx"),
    )
    return jax.shard_map(
        per_device,
        mesh=mesh,
        in_specs=placed,
        out_specs=(P("dp", "ctx", None), P()),
        check_vma=False,
    )
```

```python
import functools
import math

import jax
import jax.numpy as jnp
from jax import lax
from jax.experimental import pallas as pl
from jax.experimental.pallas import tpu as pltpu
from jax.sharding import PartitionSpec as P

QUERY_HEADS = 40
KEY_VALUE_HEADS = 8
HEAD_SIZE = 128
TOK = 192
META = 16
CAP = 7
OWNERS = 32
RING = 4
GROUP = QUERY_HEADS // KEY_VALUE_HEADS
KV_LOCAL = KEY_VALUE_HEADS // RING
Q_COLS = QUERY_HEADS * HEAD_SIZE // RING
K_COLS = KV_LOCAL * HEAD_SIZE
SLOTS = 8 * RING
WINDOW = 4 * TOK
BEHIND = 3 * TOK
LINE = 8
CHUNKS = ((0, 0, 5), (1, 5, 5))
VMEM = 60 * 1024 * 1024
MESH = pl.DeviceIdType.MESH
F32 = jnp.float32
BF16 = jnp.bfloat16


def turned_dot(a, b):
    return lax.dot_general(a, b, (((0,), (0,)), ((), ())), preferred_element_type=F32)


def dot_t(a, b):
    return lax.dot_general(a, b, (((1,), (1,)), ((), ())), preferred_element_type=F32)


def one_hot(row, count):
    iota = lax.broadcasted_iota(jnp.int32, (count, row.shape[1]), 0).astype(F32)
    return jnp.where(iota == row, 1.0, 0.0).astype(BF16)


def kernel(token_total, q, kv, cot, meta, result, curve,
           cotraw, cotp, qbuf, cbuf, kvbuf0, kvbuf1, qslots, cslots, kvslots, kvs, bias, slots, owned, acc, grads,
           parts, yparts, xparts, cparts,
           loc, kvsend, kvrecv, msend, mrecv, qsend, qrecv, csend, crecv, zsend, zrecv, ysend, yrecv, yfsend, yfrecv,
           yzsend, yzrecv, yzfsend, yzfrecv, osend, orecv, gsend, grecv, bsend, brecv, xsend, xrecv, psend, precv):
    kvbuf = (kvbuf0, kvbuf1)
    me = lax.axis_index("ctx")
    dp = lax.axis_index("dp")
    core = lax.rem(dp, 2)
    scale = 1.0 / math.sqrt(HEAD_SIZE)
    exponent = scale * math.log2(math.e)

    def turn(n):
        fast, slow = lax.rem(n, 4), n // 8
        return (slow + core * (fast - slow)) * 8 + lax.rem(n // 4, 2) * 4 + fast + core * (slow - fast)

    here = turn(me)
    x = lax.rem(here, RING)
    base = here - x
    zoff = lax.rem(here // 4, 2)
    y = here // 8
    zhere = here + 4 - 8 * zoff
    zbase = zhere - x
    line = zoff * 4 + dp // 2
    directions = (1, 3, 2)
    ways = (1, 3)

    def peer(place):
        return (dp, turn(place))

    def owner(t):
        return (dp, t)

    def line_peer(d):
        n = lax.rem(line + d, LINE)
        return (lax.rem(n, 4) * 2 + core, me + 4 * (n // 4 - zoff))

    core_peer = (dp + 1 - 2 * core, me)

    def up(d):
        return lax.rem(x + d, RING)

    def down(d):
        return lax.rem(x + RING - d, RING)

    def y_peer(d):
        return peer(lax.rem(here + 8 * d, OWNERS))

    def y_base(first, d):
        return lax.rem(first + OWNERS - 8 * d, OWNERS)

    def forward_way(i):
        return 1 if i < 2 else 3

    def send(src, dst, sems, at, device):
        return pltpu.make_async_remote_copy(
            src, dst, sems[0].at[at], sems[1].at[at], device_id=device, device_id_type=MESH)

    def kv_copy(a, d, half, to):
        return send(
            kv.at[:, pl.ds((half * RING + up(d)) * K_COLS + a * HEAD_SIZE, HEAD_SIZE)],
            kvbuf[a].at[to, pl.ds(0, TOK), pl.ds(half * HEAD_SIZE, HEAD_SIZE)],
            (kvsend, kvrecv), (a, d, half), peer(base + up(d)))

    def q_copy(c, d, to):
        _, first, count = CHUNKS[c]
        return send(
            q.at[:, pl.ds(up(d) * Q_COLS + first * HEAD_SIZE, count * HEAD_SIZE)],
            qbuf.at[to, :, pl.ds(first * HEAD_SIZE, count * HEAD_SIZE)], (qsend, qrecv), (c, d), peer(base + up(d)))

    def c_copy(c, d, to):
        _, first, count = CHUNKS[c]
        return send(
            cotp.at[:, :, pl.ds(up(d) * Q_COLS + first * HEAD_SIZE, count * HEAD_SIZE)],
            cbuf.at[to, :, :, pl.ds(first * HEAD_SIZE, count * HEAD_SIZE)], (csend, crecv), (c, d), peer(base + up(d)))

    def meta_copy(d, to):
        return send(meta, kvbuf0.at[to, pl.ds(TOK, META)], (msend, mrecv), d, peer(base + up(d)))

    def z_copy(a, i, first):
        ref = kvbuf[a].at[first + i]
        return send(ref, ref, (zsend, zrecv), (a, i), peer(zhere))

    def y_copy(a, d, first):
        ref = kvbuf[a].at[pl.ds(first, RING)]
        return send(ref, ref, (ysend, yrecv), (a, d), y_peer(d))

    def y_forward(a, d, first):
        ref = kvbuf[a].at[pl.ds(first + (0 if d == 1 else 2), 2)]
        return send(ref, ref, (yfsend, yfrecv), (a, d), y_peer(d))

    def yz_copy(a, d, i, first):
        ref = kvbuf[a].at[first + i]
        return send(ref, ref, (yzsend, yzrecv), (a, d, i), y_peer(d))

    def yz_forward(a, i, first):
        ref = kvbuf[a].at[first + i]
        return send(ref, ref, (yzfsend, yzfrecv), (a, i), y_peer(forward_way(i)))

    def place_cols(c, place):
        _, first, count = CHUNKS[c]
        return pl.ds(pl.multiple_of(lax.rem(place, RING) * Q_COLS + first * HEAD_SIZE, 128), count * HEAD_SIZE)

    def chunk_cols(c):
        _, first, count = CHUNKS[c]
        return pl.ds(first * HEAD_SIZE, count * HEAD_SIZE)

    def o_copy(c, d, target, source):
        return send(
            slots.at[target, :, chunk_cols(c)], owned.at[source // RING, :, place_cols(c, source)],
            (osend, orecv), (c, d), owner(target))

    def o_local(c):
        return pltpu.make_async_copy(
            slots.at[me, :, chunk_cols(c)], owned.at[here // RING, :, place_cols(c, here)], loc.at[c, 2])

    def kv_local(a, half):
        return pltpu.make_async_copy(
            kv.at[:, pl.ds((half * RING + x) * K_COLS + a * HEAD_SIZE, HEAD_SIZE)],
            kvbuf[a].at[here, pl.ds(0, TOK), pl.ds(half * HEAD_SIZE, HEAD_SIZE)], loc.at[a, 3 + half])

    def q_local(c):
        _, first, count = CHUNKS[c]
        return pltpu.make_async_copy(
            q.at[:, pl.ds(x * Q_COLS + first * HEAD_SIZE, count * HEAD_SIZE)], qbuf.at[x, :, chunk_cols(c)], loc.at[c, 0])

    def c_local(c):
        _, first, count = CHUNKS[c]
        return pltpu.make_async_copy(
            cotp.at[:, :, pl.ds(x * Q_COLS + first * HEAD_SIZE, count * HEAD_SIZE)],
            cbuf.at[x, :, :, chunk_cols(c)], loc.at[c, 1])

    meta_local = pltpu.make_async_copy(meta, kvbuf0.at[here, pl.ds(TOK, META)], loc.at[0, 5])

    cot_local = pltpu.make_async_copy(cot, cotraw, loc.at[1, 5])

    def tables(place):
        return kvbuf0[place, TOK: TOK + META, :].astype(F32)

    barrier = pltpu.get_barrier_semaphore()

    @pl.loop(1, OWNERS)
    def _(d):
        pl.semaphore_signal(barrier, inc=1, device_id=owner(lax.rem(me + d, OWNERS)), device_id_type=MESH)

    @pl.loop(1, LINE)
    def _(d):
        pl.semaphore_signal(barrier, inc=1, device_id=line_peer(d), device_id_type=MESH)

    pl.semaphore_signal(barrier, inc=1, device_id=core_peer, device_id_type=MESH)

    meta_local.start()
    for a in range(KV_LOCAL):
        for half in range(2):
            kv_local(a, half).start()
    for c in range(len(CHUNKS)):
        q_local(c).start()
    cot_local.start()
    acc[...] = jnp.zeros_like(acc)
    for a in range(KV_LOCAL):
        kvs[a, pl.ds(0, BEHIND), :] = jnp.zeros((BEHIND, 2 * HEAD_SIZE), BF16)
    pl.semaphore_wait(barrier, OWNERS - 1 + LINE - 1 + 1)

    for d in directions:
        for half in range(2):
            kv_copy(0, d, half, here).start()
        meta_copy(d, here).start()
    for d in directions:
        for half in range(2):
            kv_copy(1, d, half, here).start()

    def rows_of(place):
        return one_hot(tables(place)[2:3], TOK)

    def ring_rows(a, first):
        for i in range(2):
            halves = [
                turned_dot(rows_of(first + 2 * i + j), kvbuf[a][first + 2 * i + j, :TOK, :])
                .reshape(OWNERS, 8, 2 * HEAD_SIZE) for j in range(2)
            ]
            kvslots[a, :, pl.ds(pl.multiple_of(8 * first + 16 * i, 16), 16), :] = (
                jnp.concatenate(halves, axis=1).astype(BF16))

    def ring_into(c, buf, put):
        count = CHUNKS[c][2] * HEAD_SIZE

        for i in range(2):
            halves = [
                turned_dot(rows_of(base + 2 * i + j), buf(2 * i + j)).reshape(OWNERS, 8, count) for j in range(2)
            ]
            put[:, pl.ds(pl.multiple_of(16 * i, 16), 16), chunk_cols(c)] = jnp.concatenate(halves, axis=1).astype(BF16)

    def queries_in(c):
        ring_into(c, lambda s: qbuf[s, :, chunk_cols(c)], qslots)

    def cotangents_in(c):
        for p in range(2):
            ring_into(c, lambda s, p=p: cbuf[s, p, :, chunk_cols(c)], cslots.at[p])

    def wait_kv(a):
        for half in range(2):
            kv_local(a, half).wait()
        for d in directions:
            for half in range(2):
                kv_copy(a, d, half, base + down(d)).wait_recv()
            if a == 0:
                meta_copy(d, base + down(d)).wait_recv()
        if a == 0:
            meta_local.wait()

    def pass_z(a, pieces):
        for i in pieces:
            z_copy(a, i, zbase).wait_recv()
            for d in ways:
                yz_copy(a, d, i, zbase).start()

    def pass_y(a):
        for d in ways:
            y_copy(a, d, y_base(base, d)).wait_recv()
            y_forward(a, d, y_base(base, d)).start()

    def pass_yz(a):
        for i in range(RING):
            d = forward_way(i)
            yz_copy(a, d, i, y_base(zbase, d)).wait_recv()
            yz_forward(a, i, y_base(zbase, d)).start()

    slot_code = (lax.broadcasted_iota(jnp.int32, (SLOTS, TOK), 0) + base * 8).astype(F32)
    own_row = (lax.broadcasted_iota(jnp.int32, (SLOTS, TOK), 1) + BEHIND).astype(F32)
    key_at = lax.broadcasted_iota(jnp.int32, (SLOTS, WINDOW), 1).astype(F32)

    def mask(t):
        block = tables(turn(t))
        mine = slot_code == block[0:1, :TOK]
        row_at = jnp.sum(jnp.where(mine, own_row, 0.0), axis=1, keepdims=True)
        row_seg = jnp.sum(jnp.where(mine, block[1:2, :TOK], 0.0), axis=1, keepdims=True)
        key_seg = jnp.concatenate([block[:8], jnp.zeros((8, WINDOW - 256), F32)], axis=1)
        key_seg = pltpu.roll(key_seg, BEHIND, 1)
        for j in range(3):
            before = jnp.where(t + j >= 3, tables(turn(jnp.maximum(t + j - 3, 0)))[:8], 0.0)
            before = jnp.concatenate([before, jnp.zeros((8, WINDOW - 256), F32)], axis=1)
            key_seg += before if j == 0 else pltpu.roll(before, j * TOK, 1)
        allowed = (key_at <= row_at) & (key_seg[1:2] == row_seg)
        bias[t] = jnp.where(allowed, 0.0, -1e30)

    def last_keys(a):
        for i in range(RING):
            d = 4 - forward_way(i)
            yz_copy(a, d, i, y_base(zbase, d)).wait_recv()
        for d in ways:
            ring_rows(a, y_base(zbase, d))
        for d in ways:
            y_forward(a, d, y_base(base, 2)).wait_recv()
        ring_rows(a, y_base(base, 2))
        for i in range(RING):
            yz_forward(a, i, y_base(zbase, 2)).wait_recv()
        ring_rows(a, y_base(zbase, 2))

        @pl.loop(0, OWNERS // 4)
        def _(i):
            for j in range(4):
                t = 4 * i + j
                hot = one_hot(tables(turn(t))[0:1, :TOK], 256)
                kvs[a, pl.ds(pl.multiple_of(BEHIND + t * TOK, 64), TOK), :] = (
                    turned_dot(hot, kvslots[a, t]).astype(BF16))
                if a == 0:
                    mask(t)

    def wait_queries(c):
        q_local(c).wait()
        for d in directions:
            q_copy(c, d, down(d)).wait_recv()

    def wait_cotangents(c):
        c_local(c).wait()
        for d in directions:
            c_copy(c, d, down(d)).wait_recv()

    wait_kv(0)
    for i in range(RING):
        z_copy(0, i, base).start()
    for d in ways:
        y_copy(0, d, base).start()
    wait_kv(1)
    for i in range(RING):
        z_copy(1, i, base).start()

    for d in directions:
        q_copy(0, d, x).start()
    cot_local.wait()

    @pl.loop(0, TOK // 16)
    def _(i):
        rows = pl.ds(pl.multiple_of(16 * i, 16), 16)
        for p in range(2):
            cotp[p, rows, :] = cotraw[rows, p, :]

    for c in range(len(CHUNKS)):
        c_local(c).start()
    for d in directions:
        c_copy(0, d, x).start()
    ring_rows(0, base)
    pass_z(0, (0, 1))
    pass_y(0)
    pass_z(0, (2, 3))
    for d in ways:
        y_copy(1, d, base).start()
    ring_rows(0, zbase)
    for d in ways:
        ring_rows(0, y_base(base, d))

    wait_queries(0)

    pass_yz(0)
    ring_rows(1, base)
    queries_in(0)
    pass_y(1)
    pass_z(1, range(RING))
    last_keys(0)
    ring_rows(1, zbase)
    for d in ways:
        ring_rows(1, y_base(base, d))

    wait_cotangents(0)
    for d in directions:
        q_copy(1, d, x).start()
    for d in directions:
        c_copy(1, d, x).start()
    cotangents_in(0)

    def attend(c, d, u):
        a, first, count = CHUNKS[c]
        t = lax.rem(me + d, OWNERS)
        start = pl.multiple_of(t * TOK, 64)

        def heads(ref):
            return jnp.concatenate(
                [ref[t, :, h * HEAD_SIZE: (h + 1) * HEAD_SIZE] for h in range(first, first + count)], axis=0)

        keys = kvs[a, pl.ds(start, WINDOW), :HEAD_SIZE]
        values = kvs[a, pl.ds(start, WINDOW), HEAD_SIZE:]
        scores = dot_t(heads(qslots), keys).reshape(count, SLOTS, WINDOW) + bias[t][None]
        top = jnp.max(scores, axis=2, keepdims=True)
        weights = jnp.exp2((scores - top) * exponent)
        probs = weights * (1.0 / jnp.sum(weights, axis=2, keepdims=True))
        mixed = jnp.dot(probs.astype(BF16).reshape(count * SLOTS, WINDOW), values, preferred_element_type=F32)
        for h in range(count):
            slots[t, :, (first + h) * HEAD_SIZE: (first + h + 1) * HEAD_SIZE] = (
                mixed[h * SLOTS: (h + 1) * SLOTS].astype(BF16))
        sums = []
        for p in range(2):
            upstream = heads(cslots.at[p])
            delta = jnp.sum(upstream.astype(F32) * mixed, axis=1, keepdims=True)
            grad = probs * (dot_t(upstream, values) - delta).reshape(count, SLOTS, WINDOW)
            sums.append(jnp.sum(grad.reshape(count, SLOTS // 8, 8, WINDOW), axis=1).reshape(count * 8, WINDOW))
        sums = jnp.concatenate(sums, axis=0)
        high = sums.astype(BF16)
        low = (sums - high.astype(F32)).astype(BF16)
        acc[c, u, : 4 * count * 8] += jnp.dot(jnp.concatenate([high, low], axis=0), keys, preferred_element_type=F32)

    def attend_some(c, begin, end):
        @pl.loop(begin, end)
        def _(i):
            for u in range(2):
                attend(c, 2 * i + u, u)

            @pl.when(i == 0)
            def _():
                o_local(c).start()

            @pl.when(i > 0)
            def _():
                o_copy(c, 2 * i, lax.rem(me + 2 * i, OWNERS), here).start()

            o_copy(c, 2 * i + 1, lax.rem(me + 2 * i + 1, OWNERS), here).start()

    attend_some(0, 0, OWNERS // 4)
    pass_yz(1)
    attend_some(0, OWNERS // 4, OWNERS // 2)

    last_keys(1)
    for c in (1,):
        wait_queries(c)
        queries_in(c)
        wait_cotangents(c)
        cotangents_in(c)
        attend_some(c, 0, OWNERS // 2)

    grads[...] = jnp.zeros_like(grads)
    for c, (_, first, count) in enumerate(CHUNKS):
        both = acc[c, 0] + acc[c, 1]
        step = count * 8
        for p in range(2):
            total = both[p * step: (p + 1) * step] + both[(2 + p) * step: (3 + p) * step]
            for h in range(count):
                row = jnp.sum(total[h * 8: (h + 1) * 8], axis=0, keepdims=True) * scale
                grads[pl.ds(p * 16 + first + h, 1), :] = row
    parts[pl.ds(line, 1)] = grads[...][None]

    def g_copy(d, at):
        return send(parts.at[at], parts.at[at], (gsend, grecv), d, line_peer(d))

    def b_copy(d, at):
        return send(yparts.at[at], yparts.at[at], (bsend, brecv), d, y_peer(d))

    def x_copy(d, at):
        return send(xparts.at[at], xparts.at[at], (xsend, xrecv), d, peer(base + up(d)))

    def p_copy(at):
        return send(cparts.at[at], cparts.at[at], (psend, precv), 0, core_peer)

    def into_rows(c):
        hot = one_hot(tables(here)[0:1, :TOK], 256)
        o_local(c).wait()

        @pl.loop(1, OWNERS)
        def _(d):
            o_copy(c, d, me, turn(lax.rem(me + OWNERS - d, OWNERS))).wait_recv()

        _, first, count = CHUNKS[c]
        for g in range(RING):
            cols = pl.ds(g * Q_COLS + first * HEAD_SIZE, count * HEAD_SIZE)
            result[:, cols] = turned_dot(hot, owned[:, :, cols].reshape(256, count * HEAD_SIZE)).astype(BF16)

    @pl.loop(1, LINE)
    def _(d):
        g_copy(d, line).start()


    @pl.loop(1, LINE)
    def _(d):
        g_copy(d, lax.rem(line + LINE - d, LINE)).wait_recv()
        g_copy(d, line).wait_send()

    yparts[pl.ds(y, 1)] = jnp.sum(parts[...], axis=0)[None]
    for d in directions:
        b_copy(d, y).start()
    for d in directions:
        b_copy(d, lax.rem(y + RING - d, RING)).wait_recv()
        b_copy(d, y).wait_send()
    xparts[pl.ds(x, 1)] = jnp.sum(yparts[...], axis=0)[None]
    for d in directions:
        x_copy(d, x).start()
    into_rows(0)
    for d in directions:
        x_copy(d, down(d)).wait_recv()
        x_copy(d, x).wait_send()
    cparts[pl.ds(core, 1)] = xparts[...][None]
    p_copy(core).start()
    p_copy(1 - core).wait_recv()
    p_copy(core).wait_send()
    total = cparts[0] + cparts[1]
    for g in range(RING):
        square = (total[g, :16] * total[g, :16] + total[g, 16:] * total[g, 16:]) / token_total
        heads_here = QUERY_HEADS // RING
        curve[g * heads_here: (g + 1) * heads_here, :] = square[:heads_here]
    into_rows(1)

    for d in directions:
        meta_copy(d, here).wait_send()

    @pl.loop(1, OWNERS)
    def _(d):
        for c in range(len(CHUNKS)):
            o_copy(c, d, lax.rem(me + d, OWNERS), here).wait_send()

    for c in range(len(CHUNKS)):
        for d in directions:
            q_copy(c, d, x).wait_send()
            c_copy(c, d, x).wait_send()
    for a in range(KV_LOCAL):
        for d in directions:
            for half in range(2):
                kv_copy(a, d, half, here).wait_send()
        for d in ways:
            y_copy(a, d, base).wait_send()
            y_forward(a, d, y_base(base, d)).wait_send()
            for i in range(RING):
                yz_copy(a, d, i, zbase).wait_send()
        for i in range(RING):
            z_copy(a, i, base).wait_send()
            yz_forward(a, i, y_base(zbase, forward_way(i))).wait_send()


def run(q, kv, cot, meta, token_total):
    hbm = pl.BlockSpec(memory_space=pl.ANY)
    vmem = pl.BlockSpec(memory_space=pltpu.VMEM)
    n = len(CHUNKS)

    def dma(*shape):
        return [pltpu.SemaphoreType.DMA(shape)] * 2

    return pl.pallas_call(
        functools.partial(kernel, token_total),
        out_shape=(
            jax.ShapeDtypeStruct((TOK, RING * Q_COLS), BF16),
            jax.ShapeDtypeStruct((QUERY_HEADS, HEAD_SIZE), F32),
        ),
        in_specs=[hbm] * 4,
        out_specs=(vmem, vmem),
        scratch_shapes=[
            pltpu.VMEM((TOK, 2, RING * Q_COLS), BF16),
            pltpu.VMEM((2, TOK, RING * Q_COLS), BF16),
            pltpu.VMEM((RING, TOK, Q_COLS), BF16),
            pltpu.VMEM((RING, 2, TOK, Q_COLS), BF16),
            pltpu.VMEM((OWNERS, TOK + META, 2 * HEAD_SIZE), BF16),
            pltpu.VMEM((OWNERS, TOK, 2 * HEAD_SIZE), BF16),
            pltpu.VMEM((OWNERS, SLOTS, Q_COLS), BF16),
            pltpu.VMEM((2, OWNERS, SLOTS, Q_COLS), BF16),
            pltpu.VMEM((KV_LOCAL, OWNERS, 256, 2 * HEAD_SIZE), BF16),
            pltpu.VMEM((KV_LOCAL, BEHIND + OWNERS * TOK, 2 * HEAD_SIZE), BF16),
            pltpu.VMEM((OWNERS, SLOTS, WINDOW), F32),
            pltpu.VMEM((OWNERS, SLOTS, Q_COLS), BF16),
            pltpu.VMEM((OWNERS // RING, SLOTS, RING * Q_COLS), BF16),
            pltpu.VMEM((n, 2, 4 * GROUP * 8, HEAD_SIZE), F32),
            pltpu.VMEM((32, HEAD_SIZE), F32),
            pltpu.VMEM((LINE, 32, HEAD_SIZE), F32),
            pltpu.VMEM((RING, 32, HEAD_SIZE), F32),
            pltpu.VMEM((RING, 32, HEAD_SIZE), F32),
            pltpu.VMEM((2, RING, 32, HEAD_SIZE), F32),
            pltpu.SemaphoreType.DMA((n, 6)),
            *dma(KV_LOCAL, RING, 2), *dma(RING), *dma(n, RING), *dma(n, RING),
            *dma(KV_LOCAL, RING), *dma(KV_LOCAL, RING), *dma(KV_LOCAL, RING),
            *dma(KV_LOCAL, RING, RING), *dma(KV_LOCAL, RING), *dma(n, OWNERS),
            *dma(LINE), *dma(RING), *dma(RING), *dma(1),
        ],
        compiler_params=pltpu.CompilerParams(collective_id=0, has_side_effects=True, vmem_limit_bytes=VMEM),
        name="curvature",
    )(q, kv, cot, meta)


def per_device(queries, packed_keys_values, cotangents, send_rows, take_slots, segment_ids):
    sender = take_slots // CAP
    turned = (sender % 4) * 8 + (sender // 4 % 2) * 4 + sender // 8
    code = jnp.where(lax.axis_index("dp") % 2 == 0, sender, turned) * 8 + take_slots % CAP
    meta = jnp.concatenate([
        jnp.pad(code, ((0, 0), (0, 256 - TOK))),
        jnp.pad(segment_ids + 1, ((0, 0), (0, 256 - TOK))),
        jnp.pad(send_rows[0, 0], ((0, 0), (0, 8 - CAP)), constant_values=-1).reshape(1, 256),
        jnp.zeros((META - 3, 256), jnp.int32),
    ], axis=0).astype(BF16)
    token_total = 2.0 * TOK * OWNERS * lax.axis_size("dp")
    out, curve = run(queries[0], packed_keys_values[0], cotangents[0], meta, token_total)
    return out[None], curve.reshape(-1)


def solution(mesh):
    placed = (
        P("dp", "ctx", None),
        P("dp", "ctx", None),
        P("dp", "ctx", None, None),
        P("dp", "ctx", None, None),
        P("dp", "ctx"),
        P("dp", "ctx"),
    )
    return jax.shard_map(
        per_device,
        mesh=mesh,
        in_specs=placed,
        out_specs=(P("dp", "ctx", None), P()),
        check_vma=False,
    )
```
